32 devices in a mesh: fsdp: 4 (over z), context: 2 (over y), tensor: 4 (over x, core).
Axes of the slice: x: 2, y: 2, z: 4, core: 2. Of those that a mesh axis runs over, the one named last changes fastest.
Arguments:
- tokens: bfloat16 [4, 2048, 1536], P('fsdp', ('context', 'tensor')), may hold values from -6 to 6
- cotangent: bfloat16 [4, 2048, 1536], P('fsdp', ('context', 'tensor')), may hold values from -6 to 6
- segment_ids: int32 [4, 2048], P('fsdp'), may hold values from 0 to 511, as said below
- w_query: bfloat16 [1536, 1536], P(('fsdp', 'context'), 'tensor'), may hold values from -0.15625 to 0.15625
- w_keyval: bfloat16 [1536, 256], P(('fsdp', 'context', 'tensor')), may hold values from -0.15625 to 0.15625
- w_out: bfloat16 [1536, 1536], P('tensor', ('fsdp', 'context')), may hold values from -0.875 to 0.875
- w_gate: bfloat16 [1536, 4608], P(('fsdp', 'context'), 'tensor'), may hold values from -0.15625 to 0.15625
- w_up: bfloat16 [1536, 4608], P(('fsdp', 'context'), 'tensor'), may hold values from -0.15625 to 0.15625
- contract_factor: bfloat16 [4608, 1536], P('tensor', ('fsdp', 'context')), may hold values from -0.09375 to 0.09375
- norm_gains: bfloat16 [2, 1536], P(None, ('fsdp', 'context', 'tensor')), may hold values from 0.099609375 to 1.8984375
Outputs:
- output: bfloat16 [4, 2048, 1536], P('fsdp', ('context', 'tensor'))
- input_grad: float32 [4, 2048, 1536], P('fsdp', ('context', 'tensor'))
- grad_query: float32 [1536, 1536], P(('fsdp', 'context'), 'tensor')
- grad_keyval: float32 [1536, 256], P(('fsdp', 'context', 'tensor'))
- grad_out: float32 [1536, 1536], P('tensor', ('fsdp', 'context'))
- grad_gate: float32 [1536, 4608], P(('fsdp', 'context'), 'tensor')
- grad_up: float32 [1536, 4608], P(('fsdp', 'context'), 'tensor')
- grad_down: float32 [4608, 1536], P('tensor', ('fsdp', 'context'))
- grad_gains: float32 [2, 1536], P(None, ('fsdp', 'context', 'tensor'))
The draws below stay inside these ranges and needn't reach their ends.
Inputs may be any that keep to these rules, and one draw needn't show every extreme that they name: `segment_ids`: along each sequence the ids start at 0 and rise by one where a new document begins; every document but a sequence's last holds 4 tokens or more and up to 2048; one of the sequences is a single document, and another is cut into documents of 4 tokens each.
All inputs are finite; a program needn't handle non-finite values.
Results may differ from the reference program's by a relative error of at most 0.015.
Values may be sent and summed in bfloat16 or wider, within the bound.
No kernel may reach another device: no remote copies, remote signals or barrier semaphores. Data moves between devices by JAX's collectives and lax.ppermute only.
A program may use at most 192 MiB of HBM per device.

```python
import jax
import jax.numpy as jnp
from jax import lax

D = 1536
HEADS = 12
HEAD_DIM = 128
FF = 4608
WINDOW = 1024
SHARD_LEN = 1024
LENGTH = 2048
SEQS = 4
QW = 1536
N_TENSOR = 4


def draw_segment_ids(key, part):
    top_level = LENGTH.bit_length() - 1
    key_level, key_len, key_pick, key_other = jax.random.split(jax.random.fold_in(key, 17), 4)
    levels = jax.random.randint(key_level, (SEQS, LENGTH), 3, top_level + 1)
    low_end = jnp.left_shift(jnp.int32(1), levels - 1)
    lengths = jax.random.randint(key_len, (SEQS, LENGTH), low_end, 2 * low_end + 1)
    chosen = jax.random.randint(key_pick, (), 0, SEQS)
    other = (chosen + jax.random.randint(key_other, (), 1, SEQS)) % SEQS
    row_ids = jnp.arange(SEQS, dtype=jnp.int32)[:, None] + jnp.zeros((SEQS, LENGTH), jnp.int32)
    col_ids = jnp.arange(LENGTH, dtype=jnp.int32)[None, :] + jnp.zeros((SEQS, LENGTH), jnp.int32)
    lengths = jnp.where(row_ids == other, 4, lengths)
    lengths = jnp.where((row_ids == chosen) & (col_ids == 0), LENGTH, lengths)
    starts = jnp.cumsum(lengths, axis=1) - lengths
    starts = jnp.minimum(starts, LENGTH)
    doc_flags = jnp.zeros((SEQS, LENGTH + 1), jnp.int32).at[row_ids, starts].add(1)
    doc_flags = jnp.minimum(doc_flags, 1)
    document_labels = jnp.cumsum(doc_flags[:, :LENGTH], axis=1) - 1
    return document_labels.astype(jnp.int32)


def shard_levels(stream_key, dims, cuts, smallest, top_value):
    level, own = 1.0, jax.random.fold_in(stream_key, 6)
    for axis_at, parts in cuts:
        heights = jnp.exp(jax.random.uniform(jax.random.fold_in(own, axis_at), (parts,), jnp.float32, smallest / len(cuts), top_value / len(cuts)))
        level = level * jnp.repeat(heights, dims[axis_at] // parts).reshape([-1 if axis == axis_at else 1 for axis in range(len(dims))])
    return level


def scatter_about(own_key, shape, width, reach, shards=(), kind=jnp.bfloat16):
    entries = jax.random.normal(own_key, shape, jnp.float32) * width
    if len(shards) > 0:
        entries = shard_levels(own_key, shape, shards, -0.22, 0.18) * entries
    return jnp.clip(entries, min=-reach, max=reach).astype(kind)


def setup_inputs(seed: int = 0) -> dict:
    splits = jax.random.split(jax.random.key(seed), 11)
    return {
        "tokens": scatter_about(splits[0], (SEQS, LENGTH, D), 1.0, 6.0, ((0, 4), (1, 8))),
        "cotangent": scatter_about(splits[1], (SEQS, LENGTH, D), 1.0, 6.0, ((0, 4), (1, 8))),
        "segment_ids": draw_segment_ids(jax.random.fold_in(splits[10], 71), 0),
        "w_query": scatter_about(splits[3], (D, QW), D ** -0.5, 0.15625, ((0, 8), (1, 4))),
        "w_keyval": scatter_about(splits[4], (D, 2 * HEAD_DIM), D ** -0.5, 0.15625, ((0, 32),)),
        "w_out": scatter_about(splits[5], (QW, D), (QW // 32) ** -0.5, 0.875, ((0, 4), (1, 8))),
        "w_gate": scatter_about(splits[6], (D, FF), D ** -0.5, 0.15625, ((0, 8), (1, 4))),
        "w_up": scatter_about(splits[7], (D, FF), D ** -0.5, 0.15625, ((0, 8), (1, 4))),
        "contract_factor": scatter_about(splits[8], (FF, D), FF ** -0.5, 0.09375, ((0, 4), (1, 8))),
        "norm_gains": jnp.clip(1.0 + 0.18 * jax.random.normal(splits[9], (2, D), jnp.float32), 0.099609375, 1.8984375).astype(jnp.bfloat16),
    }


EPSILON = 1e-06
PRECISE = lax.Precision.HIGHEST

@jax.custom_vjp
def low(v):
    return lax.optimization_barrier(v.astype(jnp.bfloat16)).astype(jnp.float32)

@jax.custom_vjp
def low_back(v):
    return v

def low_keep(v):
    return (low(v), None)

def low_pass(kept, grad):
    return (grad,)

def back_keep(v):
    return (v, None)

def back_low(kept, grad):
    return (low(grad),)
low.defvjp(low_keep, low_pass)
low_back.defvjp(back_keep, back_low)

def rms_norm(values, gain_row):
    return values * lax.rsqrt(lax.optimization_barrier(jnp.mean(values * values, axis=-1, keepdims=True)) + EPSILON) * gain_row

def attend(queries, groups, segs):
    block_rows = min(512, SHARD_LEN)
    key_rows = block_rows + WINDOW
    group_count = N_TENSOR
    per_group = HEADS // group_count
    kv_pad = jnp.pad(groups, ((0, 0), (WINDOW, 0), (0, 0)))
    seg_pad = jnp.concatenate([jnp.full((WINDOW,), -1, jnp.int32), segs.astype(jnp.int32)])

    def one_block(block_index):
        first_token_offset = block_index * block_rows
        query_blk = lax.dynamic_slice_in_dim(queries, first_token_offset, block_rows, 0).reshape(block_rows, group_count, per_group, HEAD_DIM)
        kv_blk = lax.dynamic_slice_in_dim(kv_pad, first_token_offset, key_rows, 1)
        key_blk = kv_blk[:, :, :HEAD_DIM]
        value_blk = kv_blk[:, :, HEAD_DIM:]
        query_seg = lax.dynamic_slice_in_dim(segs.astype(jnp.int32), first_token_offset, block_rows, 0)
        key_seg = lax.dynamic_slice_in_dim(seg_pad, first_token_offset, key_rows, 0)
        query_pos = first_token_offset + jnp.arange(block_rows, dtype=jnp.int32)
        key_pos = first_token_offset - WINDOW + jnp.arange(key_rows, dtype=jnp.int32)
        allowed = (key_pos[None, :] <= query_pos[:, None]) & (key_pos[None, :] > query_pos[:, None] - WINDOW) & (key_seg[None, :] == query_seg[:, None])
        scores = jnp.einsum('qgpd,gkd->gpqk', query_blk, key_blk, precision=PRECISE) * HEAD_DIM ** (-0.5)
        scores = low_back(scores)
        scores = jnp.where(allowed[None, None], scores, -1e+30)
        row_max = lax.optimization_barrier(jnp.max(scores, axis=-1, keepdims=True))
        weights = jnp.exp(scores - row_max)
        weights = weights / lax.optimization_barrier(jnp.sum(weights, axis=-1, keepdims=True))
        mixed_out = jnp.einsum('gpqk,gkd->qgpd', low(weights), value_blk, precision=PRECISE)
        return mixed_out.reshape(block_rows, HEADS * HEAD_DIM)
    blocks = lax.map(jax.checkpoint(one_block), jnp.arange(LENGTH // block_rows, dtype=jnp.int32))
    return blocks.reshape(LENGTH, HEADS * HEAD_DIM)

def block_forward(inputs, w_query, w_keyval, w_out, w_gate, w_up, contract_factor, gains, segs):
    normed = low(rms_norm(inputs, gains[0]))
    queries = low_back(low(jnp.dot(normed, w_query, precision=PRECISE)))
    keyvals = low(jnp.dot(normed, w_keyval, precision=PRECISE))
    groups = jnp.stack([low_back(keyvals) for group_num in range(N_TENSOR)])
    head_out = low_back(low(attend(queries, groups, segs)))
    branch = low_back(jnp.dot(head_out, w_out, precision=PRECISE))
    middle = inputs + branch
    normed_two = low(rms_norm(middle, gains[1]))
    gate_pre = low_back(jnp.dot(normed_two, w_gate, precision=PRECISE))
    up_preactivation = low_back(jnp.dot(normed_two, w_up, precision=PRECISE))
    hidden_activation = low(jax.nn.gelu(gate_pre, approximate=True) * up_preactivation)
    return middle + jnp.dot(hidden_activation, contract_factor, precision=PRECISE)

def reference(tokens, cotangent, segment_ids, w_query, w_keyval, w_out, w_gate, w_up, contract_factor, norm_gains):
    params = tuple((item.astype(jnp.float32) for item in (w_query, w_keyval, w_out, w_gate, w_up, contract_factor, norm_gains)))

    def per_sequence(totals_in, inputs):
        seq_tokens, sample_derivative, segs = inputs

        def forward_fn(rows, *weight_list):
            return block_forward(rows, *weight_list, segs)
        output, chain_rule_map = jax.vjp(forward_fn, seq_tokens.astype(jnp.float32), *params)
        gradients = chain_rule_map(sample_derivative.astype(jnp.float32))
        totals_out = tuple((total + grad_item for total, grad_item in zip(totals_in, gradients[1:])))
        return (totals_out, (output.astype(jnp.bfloat16), gradients[0]))
    zeroed = tuple((jnp.zeros(item.shape, jnp.float32) for item in params))
    totals, (outputs, input_grads) = lax.scan(per_sequence, zeroed, (tokens, cotangent, segment_ids))
    return (outputs, input_grads, totals[0], totals[1], totals[2], totals[3], totals[4], totals[5], totals[6])
```

```python
import functools

import jax
import jax.numpy as jnp
from jax import lax
from jax.experimental import pallas as pl
from jax.experimental.pallas import tpu as pltpu
from jax.sharding import PartitionSpec as P

HEAD_DIM = 128
WINDOW = 1024
EPSILON = 1e-06
LOG2E = 1.4426950408889634
SCALE = HEAD_DIM**-0.5
BF = jnp.bfloat16
F32 = jnp.float32


def swap(value, axis, k):
    count = lax.axis_size(axis)
    return lax.ppermute(value, axis, [(i, i ^ k) for i in range(count)])


def shift(value, axis, steps):
    count = lax.axis_size(axis)
    leading, last = max(0, -steps), min(count, count - steps)
    return lax.ppermute(value, axis, [(i, i + steps) for i in range(leading, last)])


def bits_of(count):
    return [1 << b for b in range(count.bit_length() - 1)]


def tensor_order(count):
    order = [0]
    for bit in reversed(bits_of(count)):
        order = order + [k ^ bit for k in order]
    return order


def gather_tensor(value):
    pieces = [value]
    for bit in reversed(bits_of(lax.axis_size("tensor"))):
        pieces = pieces + [swap(p, "tensor", bit) for p in pieces]
    return jnp.concatenate(pieces, axis=0)


def reduce_tensor(make, rows):
    half = rows // 2
    away = make(half, rows).astype(BF)
    bits = bits_of(lax.axis_size("tensor"))
    back = swap(away, "tensor", bits[0])
    total = make(0, half) + back.astype(F32)
    for bit in bits[1:]:
        half //= 2
        back = swap(total[half:].astype(BF), "tensor", bit)
        total = total[:half] + back.astype(F32)
    return total


def gather_weight(shard):
    nf, nc = lax.axis_size("fsdp"), lax.axis_size("context")
    f, c = lax.axis_index("fsdp"), lax.axis_index("context")
    along = [shard] + [swap(shard, "fsdp", k) for k in range(1, nf)]
    whole = jnp.zeros((nf * nc,) + shard.shape, shard.dtype)
    for kf in range(nf):
        for kc in range(nc):
            piece = along[kf] if kc == 0 else swap(along[kf], "context", kc)
            whole = lax.dynamic_update_index_in_dim(whole, piece, (f ^ kf) * nc + (c ^ kc), 0)
    return whole.reshape(nf * nc * shard.shape[0], shard.shape[1])


def scatter_grad(part):
    nf, nc = lax.axis_size("fsdp"), lax.axis_size("context")
    f, c = lax.axis_index("fsdp"), lax.axis_index("context")
    slabs = part.reshape(nf, nc, part.shape[0] // (nf * nc), part.shape[1])
    total = lax.dynamic_index_in_dim(slabs, c, 1, False).astype(F32)
    for k in range(1, nc):
        total = total + swap(lax.dynamic_index_in_dim(slabs, c ^ k, 1, False), "context", k).astype(F32)
    own = lax.dynamic_index_in_dim(total, f, 0, False)
    for k in range(1, nf):
        sent = lax.dynamic_index_in_dim(total, f ^ k, 0, False).astype(BF)
        own = own + swap(sent, "fsdp", k).astype(F32)
    return own


def dot_nt(a, b):
    return lax.dot_general(a, b, (((1,), (1,)), ((), ())), preferred_element_type=F32)


def dot_nn(a, b):
    return lax.dot_general(a, b, (((1,), (0,)), ((), ())), preferred_element_type=F32)


def in_order(blocks_ref, prev_ref, own_ref, both, count, rows):
    for r in range(count):
        at = blocks_ref[r] * rows
        both[pl.ds(at, rows), :] = prev_ref[r * rows : (r + 1) * rows, :]
        both[pl.ds(at + count * rows, rows), :] = own_ref[r * rows : (r + 1) * rows, :]


def fill_bias(a, rows, count, qseg_ref, kseg_ref, bias, tri):
    qs = qseg_ref[...]
    wide = rows // 128

    def seg(i):
        s = kseg_ref[pl.ds((a + i) * rows, rows), :]
        return jnp.concatenate([s] * wide, axis=1) == qs

    first = (tri & seg(count)) | (jnp.logical_not(tri) & seg(0))
    bias[0] = jnp.where(first, 0.0, -1e30).astype(F32)
    for i in range(1, count):
        bias[i] = jnp.where(seg(i), 0.0, -1e30).astype(F32)


def attend_forward(blocks_ref, q_ref, prev_ref, own_ref, qseg_ref, kseg_ref, out_ref, lse_ref, both, vt, bias):
    count, rows, heads = bias.shape[0], q_ref.shape[0], q_ref.shape[1] // HEAD_DIM
    r = pl.program_id(0)
    a = blocks_ref[r]

    @pl.when(r == 0)
    def _():
        in_order(blocks_ref, prev_ref, own_ref, both, count, rows)
        for i in range(2 * count):
            vt[:, i * rows : (i + 1) * rows] = both[i * rows : (i + 1) * rows, HEAD_DIM:].T

    tri = lax.broadcasted_iota(jnp.int32, (rows, rows), 0) <= lax.broadcasted_iota(jnp.int32, (rows, rows), 1)
    fill_bias(a, rows, count, qseg_ref, kseg_ref, bias, tri)
    starts = [pl.multiple_of((a + i) * rows, rows) for i in range(count + 1)]
    for h in range(heads):
        q = q_ref[:, h * HEAD_DIM : (h + 1) * HEAD_DIM]
        s = [dot_nt(both[pl.ds(st, rows), :HEAD_DIM], q) for st in starts]
        s = [jnp.where(tri, s[count], s[0])] + s[1:count]
        s = [x * (SCALE * LOG2E) + bias[i] for i, x in enumerate(s)]
        top = functools.reduce(jnp.maximum, s)
        top = jnp.max(top, axis=0, keepdims=True)
        p = [jnp.exp2(x - top) for x in s]
        total = jnp.sum(functools.reduce(jnp.add, p), axis=0, keepdims=True)
        low = [x.astype(BF) for x in p]
        zero = jnp.zeros_like(low[0])
        low = [jnp.where(tri, zero, low[0])] + low[1:] + [jnp.where(tri, low[0], zero)]
        acc = None
        for i in range(count + 1):
            d = dot_nn(vt[:, pl.ds(starts[i], rows)], low[i])
            acc = d if acc is None else acc + d
        out_ref[:, h * HEAD_DIM : (h + 1) * HEAD_DIM] = (acc / total).T.astype(BF)
        lse_ref[h : h + 1, :] = top + jnp.log2(total)


def attend_backward(
    blocks_ref, q_ref, prev_ref, own_ref, qseg_ref, kseg_ref, dout_ref, lse_ref, dq_ref, dprev_ref, down_ref, both, kt, bias, dkv
):
    count, rows, heads = bias.shape[0], q_ref.shape[0], q_ref.shape[1] // HEAD_DIM
    r = pl.program_id(0)
    a = blocks_ref[r]

    @pl.when(r == 0)
    def _():
        in_order(blocks_ref, prev_ref, own_ref, both, count, rows)
        for i in range(2 * count):
            kt[:, i * rows : (i + 1) * rows] = both[i * rows : (i + 1) * rows, :HEAD_DIM].T
        dkv[...] = jnp.zeros_like(dkv)

    tri = lax.broadcasted_iota(jnp.int32, (rows, rows), 0) <= lax.broadcasted_iota(jnp.int32, (rows, rows), 1)
    fill_bias(a, rows, count, qseg_ref, kseg_ref, bias, tri)
    starts = [pl.multiple_of((a + i) * rows, rows) for i in range(count + 1)]
    for h in range(heads):
        cols = slice(h * HEAD_DIM, (h + 1) * HEAD_DIM)
        q, dout = q_ref[:, cols], dout_ref[:, cols]
        lse = lse_ref[h : h + 1, :]
        s = [dot_nt(both[pl.ds(st, rows), :HEAD_DIM], q) for st in starts]
        dp = [dot_nt(both[pl.ds(st, rows), HEAD_DIM:], dout) for st in starts]
        s = [jnp.where(tri, s[count], s[0])] + s[1:count]
        dp = [jnp.where(tri, dp[count], dp[0])] + dp[1:count]
        p = [jnp.exp2(x * (SCALE * LOG2E) + bias[i] - lse) for i, x in enumerate(s)]
        inner = functools.reduce(jnp.add, [x * y for x, y in zip(p, dp)])
        inner = jnp.sum(inner, axis=0, keepdims=True)
        ds = [(x * (y - inner)).astype(BF) for x, y in zip(p, dp)]
        low = [x.astype(BF) for x in p]
        zero = jnp.zeros_like(low[0])
        low = [jnp.where(tri, zero, low[0])] + low[1:] + [jnp.where(tri, low[0], zero)]
        ds = [jnp.where(tri, zero, ds[0])] + ds[1:] + [jnp.where(tri, ds[0], zero)]
        acc = None
        for i in range(count + 1):
            d = dot_nn(kt[:, pl.ds(starts[i], rows)], ds[i])
            acc = d if acc is None else acc + d
            dkv[pl.ds(starts[i], rows), :HEAD_DIM] += dot_nn(ds[i], q)
            dkv[pl.ds(starts[i], rows), HEAD_DIM:] += dot_nn(low[i], dout)
        dq_ref[:, cols] = (acc * SCALE).T.astype(BF)

    @pl.when(r == count - 1)
    def _():
        for j in range(count):
            at = blocks_ref[j] * rows
            for ref, base in ((dprev_ref, 0), (down_ref, count * rows)):
                blk = dkv[pl.ds(at + base, rows), :]
                ref[j * rows : (j + 1) * rows, :HEAD_DIM] = (blk[:, :HEAD_DIM] * SCALE).astype(ref.dtype)
                ref[j * rows : (j + 1) * rows, HEAD_DIM:] = blk[:, HEAD_DIM:].astype(ref.dtype)


def whole_spec(shape):
    return pl.BlockSpec(shape, lambda r, b: (0,) * len(shape))


def attention_forward(blocks, queries, prev, own, qseg, kseg, count):
    total, width = queries.shape
    rows = total // count
    heads = width // HEAD_DIM
    return pl.pallas_call(
        attend_forward,
        grid_spec=pltpu.PrefetchScalarGridSpec(
            num_scalar_prefetch=1,
            grid=(count,),
            in_specs=[
                pl.BlockSpec((rows, width), lambda r, b: (r, 0)),
                whole_spec(prev.shape),
                whole_spec(own.shape),
                pl.BlockSpec((1, rows), lambda r, b: (0, b[r])),
                whole_spec(kseg.shape),
            ],
            out_specs=[
                pl.BlockSpec((rows, width), lambda r, b: (r, 0)),
                pl.BlockSpec((heads, rows), lambda r, b: (0, r)),
            ],
            scratch_shapes=[
                pltpu.VMEM((2 * total, 2 * HEAD_DIM), BF),
                pltpu.VMEM((HEAD_DIM, 2 * total), BF),
                pltpu.VMEM((count, rows, rows), F32),
            ],
        ),
        out_shape=[jax.ShapeDtypeStruct((total, width), BF), jax.ShapeDtypeStruct((heads, total), F32)],
        compiler_params=pltpu.CompilerParams(vmem_limit_bytes=40 << 20),
        cost_estimate=pl.CostEstimate(flops=4 * total * WINDOW * width, bytes_accessed=6 << 20, transcendentals=heads * total * WINDOW),
        name="attend_forward",
    )(blocks, queries, prev, own, qseg, kseg)


def attention_backward(blocks, queries, prev, own, qseg, kseg, dout, lse, count):
    total, width = queries.shape
    rows = total // count
    heads = width // HEAD_DIM
    return pl.pallas_call(
        attend_backward,
        grid_spec=pltpu.PrefetchScalarGridSpec(
            num_scalar_prefetch=1,
            grid=(count,),
            in_specs=[
                pl.BlockSpec((rows, width), lambda r, b: (r, 0)),
                whole_spec(prev.shape),
                whole_spec(own.shape),
                pl.BlockSpec((1, rows), lambda r, b: (0, b[r])),
                whole_spec(kseg.shape),
                pl.BlockSpec((rows, width), lambda r, b: (r, 0)),
                pl.BlockSpec((heads, rows), lambda r, b: (0, r)),
            ],
            out_specs=[
                pl.BlockSpec((rows, width), lambda r, b: (r, 0)),
                whole_spec(prev.shape),
                whole_spec(own.shape),
            ],
            scratch_shapes=[
                pltpu.VMEM((2 * total, 2 * HEAD_DIM), BF),
                pltpu.VMEM((HEAD_DIM, 2 * total), BF),
                pltpu.VMEM((count, rows, rows), F32),
                pltpu.VMEM((2 * total, 2 * HEAD_DIM), F32),
            ],
        ),
        out_shape=[
            jax.ShapeDtypeStruct((total, width), BF),
            jax.ShapeDtypeStruct(prev.shape, BF),
            jax.ShapeDtypeStruct(own.shape, F32),
        ],
        compiler_params=pltpu.CompilerParams(vmem_limit_bytes=40 << 20),
        cost_estimate=pl.CostEstimate(flops=10 * total * WINDOW * width, bytes_accessed=10 << 20, transcendentals=heads * total * WINDOW),
        name="attend_backward",
    )(blocks, queries, prev, own, qseg, kseg, dout, lse)


def rms_inverse(values):
    return lax.rsqrt(jnp.mean(values * values, axis=-1, keepdims=True) + EPSILON)


def norm_backward(grad_normed, values, inv_rms, gain_row):
    scaled = grad_normed * gain_row
    inner_sum = jnp.mean(scaled * values, axis=-1, keepdims=True)
    return inv_rms * scaled - values * (inv_rms * inv_rms * inv_rms) * inner_sum


def mm(a, b):
    return dot_nn(a, b)


def mm_tn(a, b):
    return lax.dot_general(a, b, (((0,), (0,)), ((), ())), preferred_element_type=F32)


def local(tokens, cotangent, segment_ids, w_query, w_keyval, w_out, w_gate, w_up, w_down, norm_gains):
    nt = lax.axis_size("tensor")
    t, c = lax.axis_index("tensor"), lax.axis_index("context")
    tokens, cotangent = tokens[0], cotangent[0]
    own_rows, width = tokens.shape
    rows = own_rows * nt
    if rows != WINDOW:
        raise ValueError("shard length")
    order = tensor_order(nt)
    blocks = jnp.array(order, jnp.int32) ^ t

    token_rows = gather_tensor(tokens)
    cot_rows = gather_tensor(cotangent)

    part = w_keyval.shape[0]
    kv_cols = w_keyval.shape[1]
    small = jnp.concatenate([w_keyval, norm_gains.T, jnp.zeros((part, 126), BF)], axis=1)
    pieces = gather_tensor(small[None])
    small = jnp.zeros_like(pieces)
    for i in range(nt):
        small = lax.dynamic_update_index_in_dim(small, pieces[i], blocks[i], 0)
    small = small.reshape(nt * part, small.shape[2])
    first = gather_weight(jnp.concatenate([w_query, small], axis=1))
    qcols = w_query.shape[1]
    wq, wkv = first[:, :qcols], first[:, qcols : qcols + kv_cols]
    gains = first[:, qcols + kv_cols : qcols + kv_cols + 2].T.astype(F32)
    gain_one, gain_two = gains[0:1], gains[1:2]
    wo_t = gather_weight(w_out.T)
    wg = gather_weight(w_gate)
    wu = gather_weight(w_up)
    wd_t = gather_weight(w_down.T)

    ids = segment_ids[0]
    own_seg = lax.dynamic_slice_in_dim(ids, c * rows, rows, 0)
    prev_seg = lax.dynamic_slice_in_dim(ids, jnp.maximum(c - 1, 0) * rows, rows, 0)
    prev_seg = jnp.where(c > 0, prev_seg, -1)
    qseg = own_seg[None, :]
    kseg = jnp.broadcast_to(jnp.concatenate([prev_seg, own_seg])[:, None], (2 * rows, 128))

    xin = token_rows.astype(F32)
    inv_one_rows = rms_inverse(xin)
    normed_one = (xin * inv_one_rows * gain_one).astype(BF)
    keyvals = mm(normed_one, wkv).astype(BF)
    earlier = shift(keyvals, "context", 1)
    queries = mm(normed_one, wq).astype(BF)
    heads_out, lse = attention_forward(blocks, queries, earlier, keyvals, qseg, kseg, nt)
    branch = reduce_tensor(lambda i, j: dot_nt(heads_out[i:j], wo_t), rows)
    own_in = tokens.astype(F32)
    middle = own_in + branch
    inv_two = rms_inverse(middle)
    normed_two = (middle * inv_two * gain_two).astype(BF)
    second_rows = gather_tensor(normed_two)

    gate_pre = mm(second_rows, wg)
    up_pre = mm(second_rows, wu)
    activated, gelu_back = jax.vjp(lambda g: jax.nn.gelu(g, approximate=True), gate_pre)
    hidden = (activated * up_pre).astype(BF)
    grad_down = scatter_grad(mm_tn(cot_rows, hidden).astype(BF)).T
    d_hidden = mm(cot_rows, wd_t)
    d_gate = gelu_back(d_hidden * up_pre)[0].astype(BF)
    d_up = (d_hidden * activated).astype(BF)
    grad_gate = scatter_grad(mm_tn(second_rows, d_gate).astype(BF))
    grad_up = scatter_grad(mm_tn(second_rows, d_up).astype(BF))
    d_two = reduce_tensor(lambda i, j: dot_nt(d_gate[i:j], wg) + dot_nt(d_up[i:j], wu), rows)
    ffn = reduce_tensor(lambda i, j: dot_nt(hidden[i:j], wd_t), rows)
    output = (middle + ffn).astype(BF)

    gain_two_part = jnp.sum(d_two * middle * inv_two, axis=0, keepdims=True)
    d_middle = cotangent.astype(F32) + norm_backward(d_two, middle, inv_two, gain_two)
    back_rows = gather_tensor(d_middle.astype(BF))
    grad_out = scatter_grad(mm_tn(back_rows, heads_out).astype(BF)).T
    d_head = mm(back_rows, wo_t).astype(BF)
    dq, dprev, dkv = attention_backward(blocks, queries, earlier, keyvals, qseg, kseg, d_head, lse, nt)
    dkv = (dkv + shift(dprev, "context", -1).astype(F32)).astype(BF)
    grad_query = scatter_grad(mm_tn(normed_one, dq).astype(BF))
    d_one = reduce_tensor(lambda i, j: dot_nt(dq[i:j], wq) + dot_nt(dkv[i:j], wkv), rows)
    inv_one = rms_inverse(own_in)
    gain_one_part = jnp.sum(d_one * own_in * inv_one, axis=0, keepdims=True)
    input_grad = d_middle + norm_backward(d_one, own_in, inv_one, gain_one)

    gains_part = jnp.concatenate([gain_one_part, gain_two_part, jnp.zeros((126, width), F32)], axis=0).T
    small_part = jnp.concatenate([mm_tn(normed_one, dkv), gains_part], axis=1).astype(BF)
    mine = scatter_grad(small_part).reshape(nt, part, kv_cols + 128)
    mine = jnp.stack([lax.dynamic_index_in_dim(mine, blocks[i], 0, False) for i in range(nt)])
    mine = reduce_tensor(lambda i, j: mine[i:j], nt)[0]
    grad_keyval = mine[:, :kv_cols]
    grad_gains = mine[:, kv_cols : kv_cols + 2].T
    return (output[None], input_grad[None], grad_query, grad_keyval, grad_out, grad_gate, grad_up, grad_down, grad_gains)


def solution(mesh):
    rows = P("fsdp", ("context", "tensor"), None)
    column = P(("fsdp", "context"), "tensor")
    row = P("tensor", ("fsdp", "context"))
    small = P(("fsdp", "context", "tensor"), None)
    gains = P(None, ("fsdp", "context", "tensor"))
    return jax.shard_map(
        local,
        mesh=mesh,
        in_specs=(rows, rows, P("fsdp", None), column, small, row, column, column, row, gains),
        out_specs=(rows, rows, column, small, row, column, column, row, gains),
        check_vma=False,
    )
```

```python
import functools

import jax
import jax.numpy as jnp
from jax import lax
from jax.experimental import pallas as pl
from jax.experimental.pallas import tpu as pltpu
from jax.sharding import PartitionSpec as P

HEAD_DIM = 128
WINDOW = 1024
EPSILON = 1e-06
LOG2E = 1.4426950408889634
SCALE = HEAD_DIM**-0.5
BF = jnp.bfloat16
F32 = jnp.float32


def swap(value, axis, k):
    count = lax.axis_size(axis)
    return lax.ppermute(value, axis, [(i, i ^ k) for i in range(count)])


def shift(value, axis, steps):
    count = lax.axis_size(axis)
    leading, last = max(0, -steps), min(count, count - steps)
    return lax.ppermute(value, axis, [(i, i + steps) for i in range(leading, last)])


def bits_of(count):
    return [1 << b for b in range(count.bit_length() - 1)]


def tensor_order(count):
    order = [0]
    for bit in reversed(bits_of(count)):
        order = order + [k ^ bit for k in order]
    return order


def after(value, *deps):
    return lax.optimization_barrier((value,) + deps)[0]


def gather_tensor(value, *deps):
    pieces = [after(value, *deps) if deps else value]
    for bit in reversed(bits_of(lax.axis_size("tensor"))):
        pieces = pieces + [swap(p, "tensor", bit) for p in pieces]
    return jnp.concatenate(pieces, axis=0)


def reduce_tensor(make, rows):
    half = rows // 2
    away = make(half, rows).astype(BF)
    bits = bits_of(lax.axis_size("tensor"))
    back = swap(away, "tensor", bits[0])
    total = make(0, half) + back.astype(F32)
    for bit in bits[1:]:
        half //= 2
        back = swap(total[half:].astype(BF), "tensor", bit)
        total = total[:half] + back.astype(F32)
    return total


def gather_fsdp(shard):
    nf, f = lax.axis_size("fsdp"), lax.axis_index("fsdp")
    whole = jnp.zeros((nf,) + shard.shape, shard.dtype)
    whole = lax.dynamic_update_index_in_dim(whole, shard, f, 0)
    for k in range(1, nf):
        whole = lax.dynamic_update_index_in_dim(whole, swap(shard, "fsdp", k), f ^ k, 0)
    return whole


def gather_context(part):
    nc, c = lax.axis_size("context"), lax.axis_index("context")
    return [part] + [swap(part, "context", k) for k in range(1, nc)]


def join_context(parts):
    nc, c = lax.axis_size("context"), lax.axis_index("context")
    nf, rows, n = parts[0].shape
    whole = jnp.zeros((nf, nc, rows, n), parts[0].dtype)
    for k, part in enumerate(parts):
        whole = lax.dynamic_update_index_in_dim(whole, part, c ^ k, 1)
    return whole.reshape(nf * nc * rows, n)


def gather_weights(shards):
    done, along, parts = (), [], []
    for s in range(len(shards) + 1):
        new = ()
        if s < len(shards):
            shard = after(shards[s], *done) if done else shards[s]
            along.append(gather_fsdp(shard))
            new += (along[s],)
        if s > 0:
            part = after(along[s - 1], *done)
            parts.append(gather_context(part))
            new += tuple(parts[s - 1][1:])
        done = new
    return [join_context(p) for p in parts]


class Scatter:
    def __init__(self):
        self.last_c, self.last_f = (), ()

    def __call__(self, slabs):
        nf, nc = lax.axis_size("fsdp"), lax.axis_size("context")
        f, c = lax.axis_index("fsdp"), lax.axis_index("context")
        total = lax.dynamic_index_in_dim(slabs, c, 1, False).astype(F32)
        got = []
        for k in range(1, nc):
            sent = lax.dynamic_index_in_dim(slabs, c ^ k, 1, False)
            got.append(swap(after(sent, *self.last_c) if self.last_c else sent, "context", k))
            total = total + got[-1].astype(F32)
        self.last_c = tuple(got)
        own = lax.dynamic_index_in_dim(total, f, 0, False)
        sent = tuple(lax.dynamic_index_in_dim(total, f ^ k, 0, False).astype(BF) for k in range(1, nf))
        if self.last_f:
            sent = lax.optimization_barrier((sent, self.last_f))[0]
        got = tuple(swap(x, "fsdp", k + 1) for k, x in enumerate(sent))
        self.last_f = got
        for x in got:
            own = own + x.astype(F32)
        return own


def slabs_of(part):
    nf, nc = lax.axis_size("fsdp"), lax.axis_size("context")
    return part.reshape(nf, nc, part.shape[0] // (nf * nc), part.shape[1])


def dot_nt(a, b):
    return lax.dot_general(a, b, (((1,), (1,)), ((), ())), preferred_element_type=F32)


def dot_nn(a, b):
    return lax.dot_general(a, b, (((1,), (0,)), ((), ())), preferred_element_type=F32)


def in_order(blocks_ref, prev_ref, own_ref, both, count, rows):
    for r in range(count):
        at = blocks_ref[r] * rows
        both[pl.ds(at, rows), :] = prev_ref[r * rows : (r + 1) * rows, :]
        both[pl.ds(at + count * rows, rows), :] = own_ref[r * rows : (r + 1) * rows, :]


def fill_bias(a, rows, count, qseg_ref, kseg_ref, bias, tri):
    qs = qseg_ref[...]
    wide = rows // 128

    def seg(i):
        s = kseg_ref[pl.ds((a + i) * rows, rows), :]
        return jnp.concatenate([s] * wide, axis=1) == qs

    first = (tri & seg(count)) | (jnp.logical_not(tri) & seg(0))
    bias[0] = jnp.where(first, 0.0, -1e30).astype(F32)
    for i in range(1, count):
        bias[i] = jnp.where(seg(i), 0.0, -1e30).astype(F32)


def attend_forward(blocks_ref, q_ref, prev_ref, own_ref, qseg_ref, kseg_ref, out_ref, lse_ref, both, vt, bias):
    count, rows, heads = bias.shape[0], q_ref.shape[0], q_ref.shape[1] // HEAD_DIM
    r = pl.program_id(0)
    a = blocks_ref[r]

    @pl.when(r == 0)
    def _():
        in_order(blocks_ref, prev_ref, own_ref, both, count, rows)
        for i in range(2 * count):
            vt[:, i * rows : (i + 1) * rows] = both[i * rows : (i + 1) * rows, HEAD_DIM:].T

    tri = lax.broadcasted_iota(jnp.int32, (rows, rows), 0) <= lax.broadcasted_iota(jnp.int32, (rows, rows), 1)
    fill_bias(a, rows, count, qseg_ref, kseg_ref, bias, tri)
    starts = [pl.multiple_of((a + i) * rows, rows) for i in range(count + 1)]
    for h in range(heads):
        q = q_ref[:, h * HEAD_DIM : (h + 1) * HEAD_DIM]
        s = [dot_nt(both[pl.ds(st, rows), :HEAD_DIM], q) for st in starts]
        s = [jnp.where(tri, s[count], s[0])] + s[1:count]
        s = [x * (SCALE * LOG2E) + bias[i] for i, x in enumerate(s)]
        top = functools.reduce(jnp.maximum, s)
        top = jnp.max(top, axis=0, keepdims=True)
        p = [jnp.exp2(x - top) for x in s]
        total = jnp.sum(functools.reduce(jnp.add, p), axis=0, keepdims=True)
        low = [x.astype(BF) for x in p]
        zero = jnp.zeros_like(low[0])
        low = [jnp.where(tri, zero, low[0])] + low[1:] + [jnp.where(tri, low[0], zero)]
        acc = None
        for i in range(count + 1):
            d = dot_nn(vt[:, pl.ds(starts[i], rows)], low[i])
            acc = d if acc is None else acc + d
        out_ref[:, h * HEAD_DIM : (h + 1) * HEAD_DIM] = (acc / total).T.astype(BF)
        lse_ref[h : h + 1, :] = top + jnp.log2(total)


def attend_backward(
    blocks_ref, q_ref, prev_ref, own_ref, qseg_ref, kseg_ref, dout_ref, lse_ref, dq_ref, dprev_ref, down_ref, both, kt, bias, dkv
):
    count, rows, heads = bias.shape[0], q_ref.shape[0], q_ref.shape[1] // HEAD_DIM
    r = pl.program_id(0)
    a = blocks_ref[r]

    @pl.when(r == 0)
    def _():
        in_order(blocks_ref, prev_ref, own_ref, both, count, rows)
        for i in range(2 * count):
            kt[:, i * rows : (i + 1) * rows] = both[i * rows : (i + 1) * rows, :HEAD_DIM].T
        dkv[...] = jnp.zeros_like(dkv)

    tri = lax.broadcasted_iota(jnp.int32, (rows, rows), 0) <= lax.broadcasted_iota(jnp.int32, (rows, rows), 1)
    fill_bias(a, rows, count, qseg_ref, kseg_ref, bias, tri)
    starts = [pl.multiple_of((a + i) * rows, rows) for i in range(count + 1)]
    for h in range(heads):
        cols = slice(h * HEAD_DIM, (h + 1) * HEAD_DIM)
        q, dout = q_ref[:, cols], dout_ref[:, cols]
        lse = lse_ref[h : h + 1, :]
        s = [dot_nt(both[pl.ds(st, rows), :HEAD_DIM], q) for st in starts]
        dp = [dot_nt(both[pl.ds(st, rows), HEAD_DIM:], dout) for st in starts]
        s = [jnp.where(tri, s[count], s[0])] + s[1:count]
        dp = [jnp.where(tri, dp[count], dp[0])] + dp[1:count]
        p = [jnp.exp2(x * (SCALE * LOG2E) + bias[i] - lse) for i, x in enumerate(s)]
        inner = functools.reduce(jnp.add, [x * y for x, y in zip(p, dp)])
        inner = jnp.sum(inner, axis=0, keepdims=True)
        ds = [(x * (y - inner)).astype(BF) for x, y in zip(p, dp)]
        low = [x.astype(BF) for x in p]
        zero = jnp.zeros_like(low[0])
        low = [jnp.where(tri, zero, low[0])] + low[1:] + [jnp.where(tri, low[0], zero)]
        ds = [jnp.where(tri, zero, ds[0])] + ds[1:] + [jnp.where(tri, ds[0], zero)]
        acc = None
        for i in range(count + 1):
            d = dot_nn(kt[:, pl.ds(starts[i], rows)], ds[i])
            acc = d if acc is None else acc + d
            dkv[pl.ds(starts[i], rows), :HEAD_DIM] += dot_nn(ds[i], q)
            dkv[pl.ds(starts[i], rows), HEAD_DIM:] += dot_nn(low[i], dout)
        dq_ref[:, cols] = (acc * SCALE).T.astype(BF)

    @pl.when(r == count - 1)
    def _():
        for j in range(count):
            at = blocks_ref[j] * rows
            for ref, base in ((dprev_ref, 0), (down_ref, count * rows)):
                blk = dkv[pl.ds(at + base, rows), :]
                ref[j * rows : (j + 1) * rows, :HEAD_DIM] = (blk[:, :HEAD_DIM] * SCALE).astype(ref.dtype)
                ref[j * rows : (j + 1) * rows, HEAD_DIM:] = blk[:, HEAD_DIM:].astype(ref.dtype)


def whole_spec(shape):
    return pl.BlockSpec(shape, lambda r, b: (0,) * len(shape))


def attention_forward(blocks, queries, prev, own, qseg, kseg, count):
    total, width = queries.shape
    rows = total // count
    heads = width // HEAD_DIM
    return pl.pallas_call(
        attend_forward,
        grid_spec=pltpu.PrefetchScalarGridSpec(
            num_scalar_prefetch=1,
            grid=(count,),
            in_specs=[
                pl.BlockSpec((rows, width), lambda r, b: (r, 0)),
                whole_spec(prev.shape),
                whole_spec(own.shape),
                pl.BlockSpec((1, rows), lambda r, b: (0, b[r])),
                whole_spec(kseg.shape),
            ],
            out_specs=[
                pl.BlockSpec((rows, width), lambda r, b: (r, 0)),
                pl.BlockSpec((heads, rows), lambda r, b: (0, r)),
            ],
            scratch_shapes=[
                pltpu.VMEM((2 * total, 2 * HEAD_DIM), BF),
                pltpu.VMEM((HEAD_DIM, 2 * total), BF),
                pltpu.VMEM((count, rows, rows), F32),
            ],
        ),
        out_shape=[jax.ShapeDtypeStruct((total, width), BF), jax.ShapeDtypeStruct((heads, total), F32)],
        compiler_params=pltpu.CompilerParams(vmem_limit_bytes=40 << 20),
        cost_estimate=pl.CostEstimate(flops=4 * total * WINDOW * width, bytes_accessed=6 << 20, transcendentals=heads * total * WINDOW),
        name="attend_forward",
    )(blocks, queries, prev, own, qseg, kseg)


def attention_backward(blocks, queries, prev, own, qseg, kseg, dout, lse, count):
    total, width = queries.shape
    rows = total // count
    heads = width // HEAD_DIM
    return pl.pallas_call(
        attend_backward,
        grid_spec=pltpu.PrefetchScalarGridSpec(
            num_scalar_prefetch=1,
            grid=(count,),
            in_specs=[
                pl.BlockSpec((rows, width), lambda r, b: (r, 0)),
                whole_spec(prev.shape),
                whole_spec(own.shape),
                pl.BlockSpec((1, rows), lambda r, b: (0, b[r])),
                whole_spec(kseg.shape),
                pl.BlockSpec((rows, width), lambda r, b: (r, 0)),
                pl.BlockSpec((heads, rows), lambda r, b: (0, r)),
            ],
            out_specs=[
                pl.BlockSpec((rows, width), lambda r, b: (r, 0)),
                whole_spec(prev.shape),
                whole_spec(own.shape),
            ],
            scratch_shapes=[
                pltpu.VMEM((2 * total, 2 * HEAD_DIM), BF),
                pltpu.VMEM((HEAD_DIM, 2 * total), BF),
                pltpu.VMEM((count, rows, rows), F32),
                pltpu.VMEM((2 * total, 2 * HEAD_DIM), F32),
            ],
        ),
        out_shape=[
            jax.ShapeDtypeStruct((total, width), BF),
            jax.ShapeDtypeStruct(prev.shape, BF),
            jax.ShapeDtypeStruct(own.shape, F32),
        ],
        compiler_params=pltpu.CompilerParams(vmem_limit_bytes=40 << 20),
        cost_estimate=pl.CostEstimate(flops=10 * total * WINDOW * width, bytes_accessed=10 << 20, transcendentals=heads * total * WINDOW),
        name="attend_backward",
    )(blocks, queries, prev, own, qseg, kseg, dout, lse)


def rms_inverse(values):
    return lax.rsqrt(jnp.mean(values * values, axis=-1, keepdims=True) + EPSILON)


def norm_backward(grad_normed, values, inv_rms, gain_row):
    scaled = grad_normed * gain_row
    inner_sum = jnp.mean(scaled * values, axis=-1, keepdims=True)
    return inv_rms * scaled - values * (inv_rms * inv_rms * inv_rms) * inner_sum


def mm(a, b):
    return dot_nn(a, b)


def mm_tn(a, b):
    return lax.dot_general(a, b, (((0,), (0,)), ((), ())), preferred_element_type=F32)


def local(tokens, cotangent, segment_ids, w_query, w_keyval, w_out, w_gate, w_up, w_down, norm_gains):
    nt = lax.axis_size("tensor")
    t, c = lax.axis_index("tensor"), lax.axis_index("context")
    tokens, cotangent = tokens[0], cotangent[0]
    own_rows, width = tokens.shape
    rows = own_rows * nt
    if rows != WINDOW:
        raise ValueError("shard length")
    order = tensor_order(nt)
    blocks = jnp.array(order, jnp.int32) ^ t

    part = w_keyval.shape[0]
    kv_cols = w_keyval.shape[1]
    qcols = w_query.shape[1]
    small = jnp.concatenate([w_keyval, norm_gains.T, jnp.zeros((part, 126), BF)], axis=1)
    pieces = gather_tensor(small[None])
    small = jnp.zeros_like(pieces)
    for i in range(nt):
        small = lax.dynamic_update_index_in_dim(small, pieces[i], blocks[i], 0)
    small = small.reshape(nt * part, small.shape[2])

    token_rows = gather_tensor(tokens, pieces)
    cot_rows = gather_tensor(cotangent, token_rows)

    wo_t, first, wg, wu, wd_t = gather_weights([w_out.T, jnp.concatenate([w_query, small], axis=1), w_gate, w_up, w_down.T])
    wq, wkv = first[:, :qcols], first[:, qcols : qcols + kv_cols]
    gain_cols = first[:, qcols + kv_cols : qcols + kv_cols + 2].astype(F32)
    gains = gain_cols.T
    gain_one, gain_two = gains[0:1], gains[1:2]

    ids = segment_ids[0]
    own_seg = lax.dynamic_slice_in_dim(ids, c * rows, rows, 0)
    prev_seg = lax.dynamic_slice_in_dim(ids, jnp.maximum(c - 1, 0) * rows, rows, 0)
    prev_seg = jnp.where(c > 0, prev_seg, -1)
    qseg = own_seg[None, :]
    kseg = jnp.broadcast_to(jnp.concatenate([prev_seg, own_seg])[:, None], (2 * rows, 128))

    xin = token_rows.astype(F32)
    inv_one_rows = rms_inverse(xin)
    normed_one = (xin * inv_one_rows * gain_one).astype(BF)
    keyvals = mm(normed_one, wkv).astype(BF)
    earlier = shift(keyvals, "context", 1)
    queries = mm(normed_one, wq).astype(BF)
    heads_out, lse = attention_forward(blocks, queries, earlier, keyvals, qseg, kseg, nt)
    branch = reduce_tensor(lambda i, j: dot_nt(heads_out[i:j], wo_t), rows)
    own_in = tokens.astype(F32)
    middle = own_in + branch
    inv_two = rms_inverse(middle)
    normed_two = (middle * inv_two * gain_two).astype(BF)
    second_rows = gather_tensor(normed_two)

    scatter = Scatter()
    gate_pre = mm(second_rows, wg)
    up_pre = mm(second_rows, wu)
    activated, gelu_back = jax.vjp(lambda g: jax.nn.gelu(g, approximate=True), gate_pre)
    hidden = (activated * up_pre).astype(BF)
    grad_down = scatter(slabs_of(mm_tn(cot_rows, hidden).astype(BF))).T
    d_hidden = mm(cot_rows, wd_t)
    d_gate = gelu_back(d_hidden * up_pre)[0].astype(BF)
    d_up = (d_hidden * activated).astype(BF)
    grad_gate = scatter(slabs_of(mm_tn(second_rows, d_gate).astype(BF)))
    grad_up = scatter(slabs_of(mm_tn(second_rows, d_up).astype(BF)))
    d_two = reduce_tensor(lambda i, j: dot_nt(d_gate[i:j], wg) + dot_nt(d_up[i:j], wu), rows)

    gain_two_part = jnp.sum(d_two * middle * inv_two, axis=0, keepdims=True)
    d_middle = cotangent.astype(F32) + norm_backward(d_two, middle, inv_two, gain_two)
    back_rows = gather_tensor(d_middle.astype(BF))
    ffn = reduce_tensor(lambda i, j: dot_nt(after(hidden, back_rows)[i:j], wd_t), rows)
    output = (middle + ffn).astype(BF)
    grad_out = scatter(slabs_of(mm_tn(back_rows, heads_out).astype(BF))).T
    d_head = mm(back_rows, wo_t).astype(BF)
    dq, dprev, dkv = attention_backward(blocks, queries, earlier, keyvals, qseg, kseg, d_head, lse, nt)
    dkv = (dkv + shift(dprev, "context", -1).astype(F32)).astype(BF)
    d_one = reduce_tensor(lambda i, j: dot_nt(dq[i:j], wq) + dot_nt(dkv[i:j], wkv), rows)
    inv_one = rms_inverse(own_in)
    input_grad = d_middle + norm_backward(d_one, own_in, inv_one, gain_one)

    query_part = mm_tn(normed_one, dq)
    kv_part = mm_tn(normed_one, dkv)
    gain_one_part = jnp.sum(query_part * wq.astype(F32), axis=1, keepdims=True) + jnp.sum(kv_part * wkv.astype(F32), axis=1, keepdims=True)
    gain_one_part = gain_one_part / gain_cols[:, 0:1]
    small_part = jnp.concatenate([kv_part, gain_one_part, gain_two_part.T, jnp.zeros((width, 126), F32)], axis=1)
    small_part = small_part.reshape(-1, nt, part, kv_cols + 128)
    small_part = jnp.stack([lax.dynamic_index_in_dim(small_part, blocks[i], 1, False) for i in range(nt)])
    small_part = reduce_tensor(lambda i, j: small_part[i:j], nt)[0].astype(BF)
    nf, nc = lax.axis_size("fsdp"), lax.axis_size("context")
    last = jnp.concatenate([slabs_of(query_part.astype(BF)), small_part.reshape(nf, nc, part, kv_cols + 128)], axis=2)
    last = scatter(last)
    grad_query, small_sum = last[: nt * part], last[nt * part :]
    grad_keyval = small_sum[:, :kv_cols]
    grad_gains = small_sum[:, kv_cols : kv_cols + 2].T
    return (output[None], input_grad[None], grad_query, grad_keyval, grad_out, grad_gate, grad_up, grad_down, grad_gains)


def solution(mesh):
    rows = P("fsdp", ("context", "tensor"), None)
    column = P(("fsdp", "context"), "tensor")
    row = P("tensor", ("fsdp", "context"))
    small = P(("fsdp", "context", "tensor"), None)
    gains = P(None, ("fsdp", "context", "tensor"))
    return jax.shard_map(
        local,
        mesh=mesh,
        in_specs=(rows, rows, P("fsdp", None), column, small, row, column, column, row, gains),
        out_specs=(rows, rows, column, small, row, column, column, row, gains),
        check_vma=False,
    )
```

```python
import functools

import jax
import jax.numpy as jnp
from jax import lax
from jax.experimental import pallas as pl
from jax.experimental.pallas import tpu as pltpu
from jax.sharding import PartitionSpec as P

HEAD_DIM = 128
WINDOW = 1024
EPSILON = 1e-06
LOG2E = 1.4426950408889634
SCALE = HEAD_DIM**-0.5
BF = jnp.bfloat16
F32 = jnp.float32


def swap(value, axis, k):
    count = lax.axis_size(axis)
    return lax.ppermute(value, axis, [(i, i ^ k) for i in range(count)])


def shift(value, axis, steps):
    count = lax.axis_size(axis)
    leading, last = max(0, -steps), min(count, count - steps)
    return lax.ppermute(value, axis, [(i, i + steps) for i in range(leading, last)])


def bits_of(count):
    return [1 << b for b in range(count.bit_length() - 1)]


def tensor_order(count):
    order = [0]
    for bit in reversed(bits_of(count)):
        order = order + [k ^ bit for k in order]
    return order


def after(value, *deps):
    return lax.optimization_barrier((value,) + deps)[0]


def tensor_blocks(value, first=(), later=()):
    pieces = behind([value], *first)
    bits = list(reversed(bits_of(lax.axis_size("tensor"))))
    for n, bit in enumerate(bits):
        if n == len(bits) - 1 and later:
            pieces = behind(pieces, *later)
        pieces = pieces + [swap(p, "tensor", bit) for p in pieces]
    return pieces


def reduce_halves(away, own):
    bits = bits_of(lax.axis_size("tensor"))
    back = swap(away.astype(BF), "tensor", bits[0])
    total = own + back.astype(F32)
    for bit in bits[1:]:
        half = total.shape[0] // 2
        back = swap(total[half:].astype(BF), "tensor", bit)
        total = total[:half] + back.astype(F32)
    return total


def reduce_tensor(make, rows):
    half = rows // 2
    return reduce_halves(make(half, rows), make(0, half))


def behind(values, *deps):
    return list(lax.optimization_barrier((tuple(values), deps))[0])


def across(value, *deps):
    (value,) = behind([value], *deps)
    return [swap(value, "context", k) for k in range(1, lax.axis_size("context"))]


def along(value, *deps):
    (value,) = behind([value], *deps)
    return [swap(value, "fsdp", k) for k in range(1, lax.axis_size("fsdp"))]


def place_kernel(cuts, slots, *refs):
    n_out = len(cuts)
    ins, outs, sems = refs[: -n_out - 1], refs[-n_out - 1 : -1], refs[-1]
    copies, n = [], 0
    for ref in ins:
        for i in range(ref.shape[0]):
            for out, (first, last) in zip(outs, cuts):
                copies.append(pltpu.make_async_copy(ref.at[i, first:last], out.at[slots[n]], sems.at[len(copies)]))
                copies[-1].start()
            n += 1
    for copy in copies:
        copy.wait()


def place(slots, pieces, cuts=None):
    count = sum(p.shape[0] for p in pieces)
    rows, n = pieces[0].shape[1:]
    cuts = cuts or [(0, rows)]
    anywhere = pl.BlockSpec(memory_space=pl.ANY)
    shapes = [(count, last - first, n) for first, last in cuts]
    out = pl.pallas_call(
        functools.partial(place_kernel, cuts),
        grid_spec=pltpu.PrefetchScalarGridSpec(
            num_scalar_prefetch=1,
            grid=(1,),
            in_specs=[anywhere] * len(pieces),
            out_specs=[whole_spec(shape) for shape in shapes],
            scratch_shapes=[pltpu.SemaphoreType.DMA((count * len(cuts),))],
        ),
        out_shape=[jax.ShapeDtypeStruct(shape, pieces[0].dtype) for shape in shapes],
        cost_estimate=pl.CostEstimate(flops=1, bytes_accessed=1, transcendentals=0),
        name="place",
    )(slots, *pieces)
    return [x.reshape(-1, n) for x in out]


def gathered(own, others, early, later):
    pieces = [own[None], others]
    for e, a in zip(early, later):
        pieces += [e[None], a]
    return pieces


def slots_of():
    nf, nc = lax.axis_size("fsdp"), lax.axis_size("context")
    f, c = lax.axis_index("fsdp"), lax.axis_index("context")
    js = jnp.array([j for _ in range(nc) for j in range(nf)], jnp.int32)
    ks = jnp.array([k for k in range(nc) for _ in range(nf)], jnp.int32)
    return (js ^ f) * nc + (ks ^ c)


def half_sent(slabs, *deps):
    c = lax.axis_index("context")
    out = []
    for k in range(1, lax.axis_size("context")):
        (sent,) = behind([lax.dynamic_index_in_dim(slabs, c ^ k, 1, False)], *deps)
        out.append(swap(sent, "context", k))
    return out


def half_sum(slabs, got):
    return lax.dynamic_index_in_dim(slabs, lax.axis_index("context"), 1, False).astype(F32) + sum(x.astype(F32) for x in got)


def rest_large(total):
    return lax.psum_scatter(total.astype(BF), "fsdp", scatter_dimension=0, tiled=False).astype(F32)


def rest_small(total, *deps):
    nf, f = lax.axis_size("fsdp"), lax.axis_index("fsdp")
    away = behind([lax.dynamic_index_in_dim(total, f ^ k, 0, False).astype(BF) for k in range(1, nf)], *deps)
    back = [swap(x, "fsdp", k + 1) for k, x in enumerate(away)]
    return lax.dynamic_index_in_dim(total, f, 0, False) + sum(x.astype(F32) for x in back), back


def slabs_of(part):
    nf, nc = lax.axis_size("fsdp"), lax.axis_size("context")
    return part.reshape(nf, nc, part.shape[0] // (nf * nc), part.shape[1])


def dot_nt(a, b):
    return lax.dot_general(a, b, (((1,), (1,)), ((), ())), preferred_element_type=F32)


def dot_nn(a, b):
    return lax.dot_general(a, b, (((1,), (0,)), ((), ())), preferred_element_type=F32)


def in_order(blocks_ref, prev_ref, own_ref, both, count, rows):
    for r in range(count):
        at = blocks_ref[r] * rows
        both[pl.ds(at, rows), :] = prev_ref[r * rows : (r + 1) * rows, :]
        both[pl.ds(at + count * rows, rows), :] = own_ref[r * rows : (r + 1) * rows, :]


def fill_bias(a, rows, count, qseg_ref, kseg_ref, bias, tri):
    qs = qseg_ref[...]
    wide = rows // 128

    def seg(i):
        s = kseg_ref[pl.ds((a + i) * rows, rows), :]
        return jnp.concatenate([s] * wide, axis=1) == qs

    first = (tri & seg(count)) | (jnp.logical_not(tri) & seg(0))
    bias[0] = jnp.where(first, 0.0, -1e30).astype(F32)
    for i in range(1, count):
        bias[i] = jnp.where(seg(i), 0.0, -1e30).astype(F32)


def attend_forward(blocks_ref, q_ref, prev_ref, own_ref, qseg_ref, kseg_ref, out_ref, lse_ref, both, vt, bias):
    count, rows, heads = bias.shape[0], q_ref.shape[0], q_ref.shape[1] // HEAD_DIM
    r = pl.program_id(0)
    a = blocks_ref[r]

    @pl.when(r == 0)
    def _():
        in_order(blocks_ref, prev_ref, own_ref, both, count, rows)
        for i in range(2 * count):
            vt[:, i * rows : (i + 1) * rows] = both[i * rows : (i + 1) * rows, HEAD_DIM:].T

    tri = lax.broadcasted_iota(jnp.int32, (rows, rows), 0) <= lax.broadcasted_iota(jnp.int32, (rows, rows), 1)
    fill_bias(a, rows, count, qseg_ref, kseg_ref, bias, tri)
    starts = [pl.multiple_of((a + i) * rows, rows) for i in range(count + 1)]
    for h in range(heads):
        q = q_ref[:, h * HEAD_DIM : (h + 1) * HEAD_DIM]
        s = [dot_nt(both[pl.ds(st, rows), :HEAD_DIM], q) for st in starts]
        s = [jnp.where(tri, s[count], s[0])] + s[1:count]
        s = [x * (SCALE * LOG2E) + bias[i] for i, x in enumerate(s)]
        top = functools.reduce(jnp.maximum, s)
        top = jnp.max(top, axis=0, keepdims=True)
        p = [jnp.exp2(x - top) for x in s]
        total = jnp.sum(functools.reduce(jnp.add, p), axis=0, keepdims=True)
        low = [x.astype(BF) for x in p]
        zero = jnp.zeros_like(low[0])
        low = [jnp.where(tri, zero, low[0])] + low[1:] + [jnp.where(tri, low[0], zero)]
        acc = None
        for i in range(count + 1):
            d = dot_nn(vt[:, pl.ds(starts[i], rows)], low[i])
            acc = d if acc is None else acc + d
        out_ref[:, h * HEAD_DIM : (h + 1) * HEAD_DIM] = (acc / total).T.astype(BF)
        lse_ref[h : h + 1, :] = top + jnp.log2(total)


def attend_backward(
    blocks_ref, q_ref, prev_ref, own_ref, qseg_ref, kseg_ref, dout_ref, lse_ref, dq_ref, dprev_ref, down_ref, both, kt, bias, dkv
):
    count, rows, heads = bias.shape[0], q_ref.shape[0], q_ref.shape[1] // HEAD_DIM
    r = pl.program_id(0)
    a = blocks_ref[r]

    @pl.when(r == 0)
    def _():
        in_order(blocks_ref, prev_ref, own_ref, both, count, rows)
        for i in range(2 * count):
            kt[:, i * rows : (i + 1) * rows] = both[i * rows : (i + 1) * rows, :HEAD_DIM].T
        dkv[...] = jnp.zeros_like(dkv)

    tri = lax.broadcasted_iota(jnp.int32, (rows, rows), 0) <= lax.broadcasted_iota(jnp.int32, (rows, rows), 1)
    fill_bias(a, rows, count, qseg_ref, kseg_ref, bias, tri)
    starts = [pl.multiple_of((a + i) * rows, rows) for i in range(count + 1)]
    for h in range(heads):
        cols = slice(h * HEAD_DIM, (h + 1) * HEAD_DIM)
        q, dout = q_ref[:, cols], dout_ref[:, cols]
        lse = lse_ref[h : h + 1, :]
        s = [dot_nt(both[pl.ds(st, rows), :HEAD_DIM], q) for st in starts]
        dp = [dot_nt(both[pl.ds(st, rows), HEAD_DIM:], dout) for st in starts]
        s = [jnp.where(tri, s[count], s[0])] + s[1:count]
        dp = [jnp.where(tri, dp[count], dp[0])] + dp[1:count]
        p = [jnp.exp2(x * (SCALE * LOG2E) + bias[i] - lse) for i, x in enumerate(s)]
        inner = functools.reduce(jnp.add, [x * y for x, y in zip(p, dp)])
        inner = jnp.sum(inner, axis=0, keepdims=True)
        ds = [(x * (y - inner)).astype(BF) for x, y in zip(p, dp)]
        low = [x.astype(BF) for x in p]
        zero = jnp.zeros_like(low[0])
        low = [jnp.where(tri, zero, low[0])] + low[1:] + [jnp.where(tri, low[0], zero)]
        ds = [jnp.where(tri, zero, ds[0])] + ds[1:] + [jnp.where(tri, ds[0], zero)]
        acc = None
        for i in range(count + 1):
            d = dot_nn(kt[:, pl.ds(starts[i], rows)], ds[i])
            acc = d if acc is None else acc + d
            dkv[pl.ds(starts[i], rows), :HEAD_DIM] += dot_nn(ds[i], q)
            dkv[pl.ds(starts[i], rows), HEAD_DIM:] += dot_nn(low[i], dout)
        dq_ref[:, cols] = (acc * SCALE).T.astype(BF)

    @pl.when(r == count - 1)
    def _():
        for j in range(count):
            at = blocks_ref[j] * rows
            for ref, base in ((dprev_ref, 0), (down_ref, count * rows)):
                blk = dkv[pl.ds(at + base, rows), :]
                ref[j * rows : (j + 1) * rows, :HEAD_DIM] = (blk[:, :HEAD_DIM] * SCALE).astype(ref.dtype)
                ref[j * rows : (j + 1) * rows, HEAD_DIM:] = blk[:, HEAD_DIM:].astype(ref.dtype)


def whole_spec(shape):
    return pl.BlockSpec(shape, lambda r, b: (0,) * len(shape))


def attention_forward(blocks, queries, prev, own, qseg, kseg, count):
    total, width = queries.shape
    rows = total // count
    heads = width // HEAD_DIM
    return pl.pallas_call(
        attend_forward,
        grid_spec=pltpu.PrefetchScalarGridSpec(
            num_scalar_prefetch=1,
            grid=(count,),
            in_specs=[
                pl.BlockSpec((rows, width), lambda r, b: (r, 0)),
                whole_spec(prev.shape),
                whole_spec(own.shape),
                pl.BlockSpec((1, rows), lambda r, b: (0, b[r])),
                whole_spec(kseg.shape),
            ],
            out_specs=[
                pl.BlockSpec((rows, width), lambda r, b: (r, 0)),
                pl.BlockSpec((heads, rows), lambda r, b: (0, r)),
            ],
            scratch_shapes=[
                pltpu.VMEM((2 * total, 2 * HEAD_DIM), BF),
                pltpu.VMEM((HEAD_DIM, 2 * total), BF),
                pltpu.VMEM((count, rows, rows), F32),
            ],
        ),
        out_shape=[jax.ShapeDtypeStruct((total, width), BF), jax.ShapeDtypeStruct((heads, total), F32)],
        compiler_params=pltpu.CompilerParams(vmem_limit_bytes=40 << 20),
        cost_estimate=pl.CostEstimate(flops=1, bytes_accessed=1, transcendentals=0),
        name="attend_forward",
    )(blocks, queries, prev, own, qseg, kseg)


def attention_backward(blocks, queries, prev, own, qseg, kseg, dout, lse, count):
    total, width = queries.shape
    rows = total // count
    heads = width // HEAD_DIM
    return pl.pallas_call(
        attend_backward,
        grid_spec=pltpu.PrefetchScalarGridSpec(
            num_scalar_prefetch=1,
            grid=(count,),
            in_specs=[
                pl.BlockSpec((rows, width), lambda r, b: (r, 0)),
                whole_spec(prev.shape),
                whole_spec(own.shape),
                pl.BlockSpec((1, rows), lambda r, b: (0, b[r])),
                whole_spec(kseg.shape),
                pl.BlockSpec((rows, width), lambda r, b: (r, 0)),
                pl.BlockSpec((heads, rows), lambda r, b: (0, r)),
            ],
            out_specs=[
                pl.BlockSpec((rows, width), lambda r, b: (r, 0)),
                whole_spec(prev.shape),
                whole_spec(own.shape),
            ],
            scratch_shapes=[
                pltpu.VMEM((2 * total, 2 * HEAD_DIM), BF),
                pltpu.VMEM((HEAD_DIM, 2 * total), BF),
                pltpu.VMEM((count, rows, rows), F32),
                pltpu.VMEM((2 * total, 2 * HEAD_DIM), F32),
            ],
        ),
        out_shape=[
            jax.ShapeDtypeStruct((total, width), BF),
            jax.ShapeDtypeStruct(prev.shape, BF),
            jax.ShapeDtypeStruct(own.shape, F32),
        ],
        compiler_params=pltpu.CompilerParams(vmem_limit_bytes=40 << 20),
        cost_estimate=pl.CostEstimate(flops=1, bytes_accessed=1, transcendentals=0),
        name="attend_backward",
    )(blocks, queries, prev, own, qseg, kseg, dout, lse)


def gelu_parts(g):
    root = 0.7978845608028654
    inner = jnp.tanh(root * (g + 0.044715 * (g * g * g)))
    half = 0.5 * (1.0 + inner)
    slope = half + 0.5 * g * (1.0 - inner * inner) * (root * (1.0 + 3 * 0.044715 * (g * g)))
    return g * half, slope


def ffn_forward_kernel(nx, *refs):
    xs, cs, (gate, up) = refs[:nx], refs[nx : 2 * nx], refs[2 * nx : 2 * nx + 2]
    hid, act, pg, x_out, c_out, x_all, c_all, sems, o_sems = refs[2 * nx + 2 :]
    rows, n = xs[0].shape[0], gate.shape[1]
    i = pl.program_id(0)
    outs = [pltpu.make_async_copy(src, dst, o_sems.at[j]) for j, (src, dst) in enumerate(((x_all, x_out), (c_all, c_out)))]

    @pl.when(i == 0)
    def _():
        copies = []
        for j, (x, y) in enumerate(zip(xs, cs)):
            copies.append(pltpu.make_async_copy(x, x_all.at[pl.ds(j * rows, rows)], sems.at[j]))
            copies[-1].start()
            copies.append(pltpu.make_async_copy(y, c_all.at[pl.ds(j * rows, rows)], sems.at[nx + j]))
            copies[-1].start()
        for c in copies:
            c.wait()
        for o in outs:
            o.start()

    x = x_all[pl.ds(pl.multiple_of(i * rows, rows), rows), :]
    step = n // 3 if n % 384 == 0 else n
    for j in range(0, n, step):
        g = dot_nn(x, gate[:, j : j + step])
        u = dot_nn(x, up[:, j : j + step])
        value, slope = gelu_parts(g)
        hid[:, j : j + step] = (value * u).astype(BF)
        act[:, j : j + step] = value.astype(BF)
        pg[:, j : j + step] = (slope * u).astype(BF)

    @pl.when(i == pl.num_programs(0) - 1)
    def _():
        for o in outs:
            o.wait()


def ffn_forward(x_blocks, c_blocks, gate, up):
    rows, width = x_blocks[0].shape
    count, n = len(x_blocks), gate.shape[1]
    total = count * rows
    anywhere = pl.BlockSpec(memory_space=pl.ANY)
    block = pl.BlockSpec((rows, n), lambda i: (i, 0))
    weight = pl.BlockSpec(gate.shape, lambda i: (0, 0))
    kept = jax.ShapeDtypeStruct((total, n), BF)
    return pl.pallas_call(
        functools.partial(ffn_forward_kernel, count),
        grid=(count,),
        in_specs=[anywhere] * (2 * count) + [weight, weight],
        out_specs=[block] * 3 + [anywhere] * 2,
        scratch_shapes=[
            pltpu.VMEM((total, width), BF),
            pltpu.VMEM((total, width), BF),
            pltpu.SemaphoreType.DMA((2 * count,)),
            pltpu.SemaphoreType.DMA((2,)),
        ],
        out_shape=[kept] * 3 + [jax.ShapeDtypeStruct((total, width), BF)] * 2,
        compiler_params=pltpu.CompilerParams(vmem_limit_bytes=48 << 20),
        cost_estimate=pl.CostEstimate(flops=4 * total * width * n, bytes_accessed=20 << 20, transcendentals=total * n),
        name="ffn_forward",
    )(*x_blocks, *c_blocks, gate, up)


def ffn_backward_kernel(cot, act, pg, down, d_gate, d_up):
    n = down.shape[1]
    x = cot[...]
    step = n // 3 if n % 384 == 0 else n
    for j in range(0, n, step):
        d = dot_nn(x, down[:, j : j + step])
        d_gate[:, j : j + step] = (d * pg[:, j : j + step].astype(F32)).astype(BF)
        d_up[:, j : j + step] = (d * act[:, j : j + step].astype(F32)).astype(BF)


def ffn_backward(cot, act, pg, down, count):
    total, width = cot.shape
    n = down.shape[1]
    rows = total // count
    block = pl.BlockSpec((rows, n), lambda i: (i, 0))
    kept = jax.ShapeDtypeStruct((total, n), BF)
    return pl.pallas_call(
        ffn_backward_kernel,
        grid=(count,),
        in_specs=[pl.BlockSpec((rows, width), lambda i: (i, 0)), block, block, pl.BlockSpec(down.shape, lambda i: (0, 0))],
        out_specs=[block, block],
        out_shape=[kept, kept],
        compiler_params=pltpu.CompilerParams(vmem_limit_bytes=40 << 20),
        cost_estimate=pl.CostEstimate(flops=2 * total * width * n, bytes_accessed=16 << 20, transcendentals=0),
        name="ffn_backward",
    )(cot, act, pg, down)


def rms_inverse(values):
    return lax.rsqrt(jnp.mean(values * values, axis=-1, keepdims=True) + EPSILON)


def norm_backward(grad_normed, values, inv_rms, gain_row):
    scaled = grad_normed * gain_row
    inner_sum = jnp.mean(scaled * values, axis=-1, keepdims=True)
    return inv_rms * scaled - values * (inv_rms * inv_rms * inv_rms) * inner_sum


def mm(a, b):
    return dot_nn(a, b)


def mm_tn(a, b):
    return lax.dot_general(a, b, (((0,), (0,)), ((), ())), preferred_element_type=F32)


def local(tokens, cotangent, segment_ids, w_query, w_keyval, w_out, w_gate, w_up, w_down, norm_gains):
    nt = lax.axis_size("tensor")
    t, c = lax.axis_index("tensor"), lax.axis_index("context")
    tokens, cotangent = tokens[0], cotangent[0]
    own_rows, width = tokens.shape
    rows = own_rows * nt
    if rows != WINDOW:
        raise ValueError("shard length")
    order = tensor_order(nt)
    blocks = jnp.array(order, jnp.int32) ^ t

    part = w_keyval.shape[0]
    kv_cols = w_keyval.shape[1]
    nf, nc = lax.axis_size("fsdp"), lax.axis_size("context")
    small_own = jnp.concatenate([w_keyval, norm_gains.T, jnp.zeros((part, 126), BF)], axis=1)
    first_own = jnp.concatenate([w_query, small_own], axis=0)
    wo_own, wd_own = w_out.T, w_down.T
    slots = slots_of()
    both = ("fsdp", "context")

    first_along = along(first_own)
    first_early = across(first_own)
    token_blocks = tensor_blocks(tokens)
    wg = lax.all_gather(w_gate, both, axis=0, tiled=True)
    first_along = jnp.stack(first_along)
    first_across = across(first_along, first_early)
    wu = lax.all_gather(after(w_up, *first_across), both, axis=0, tiled=True)
    wo_along = along(wo_own, first_along)
    wo_all = jnp.stack([wo_own, *wo_along])
    wo_across = across(wo_all, first_across)
    wd_t = lax.all_gather(after(wd_own, *wo_across), both, axis=0, tiled=True)

    own_rows_q = nt * part
    wq, small = place(slots, gathered(first_own, first_along, first_early, first_across), [(0, own_rows_q), (own_rows_q, own_rows_q + part)])
    small_blocks = tensor_blocks(small.reshape(nf * nc, part, -1))
    cot_blocks = tensor_blocks(cotangent, small_blocks)
    small = jnp.zeros((nf * nc, nt, part, small.shape[1]), BF)
    for i in range(nt):
        small = lax.dynamic_update_index_in_dim(small, small_blocks[i], t ^ order[i], 1)
    small = small.reshape(width, -1)
    wkv = small[:, :kv_cols]
    gain_cols = small[:, kv_cols : kv_cols + 2].astype(F32)
    gains = gain_cols.T
    gain_one, gain_two = gains[0:1], gains[1:2]

    ids = segment_ids[0]
    own_seg = lax.dynamic_slice_in_dim(ids, c * rows, rows, 0)
    prev_seg = lax.dynamic_slice_in_dim(ids, jnp.maximum(c - 1, 0) * rows, rows, 0)
    prev_seg = jnp.where(c > 0, prev_seg, -1)
    qseg = own_seg[None, :]
    kseg = jnp.broadcast_to(jnp.concatenate([prev_seg, own_seg])[:, None], (2 * rows, 128))

    xin = jnp.concatenate(token_blocks, axis=0).astype(F32)
    inv_one_rows = rms_inverse(xin)
    normed_one = (xin * inv_one_rows * gain_one).astype(BF)
    keyvals = mm(normed_one, wkv).astype(BF)
    earlier = shift(keyvals, "context", 1)
    queries = mm(normed_one, wq).astype(BF)
    heads_out, lse = attention_forward(blocks, after(queries, cot_blocks[1]), earlier, keyvals, qseg, kseg, nt)
    (wo_t,) = place(slots, [wo_all] + behind(wo_across, heads_out))
    heads_now = heads_out
    branch = reduce_tensor(lambda i, j: dot_nt(heads_now[i:j], wo_t), rows)
    own_in = tokens.astype(F32)
    middle = own_in + branch
    inv_two = rms_inverse(middle)
    normed_two = (middle * inv_two * gain_two).astype(BF)
    second_blocks = tensor_blocks(normed_two)

    hidden, act, pg, second_rows, cot_rows = ffn_forward(second_blocks, cot_blocks, wg, wu)
    part_down = slabs_of(mm_tn(cot_rows, hidden).astype(BF))
    got_down = half_sent(part_down)
    d_gate, d_up = ffn_backward(after(cot_rows, part_down), act, pg, wd_t, nt)
    half = rows // 2
    two_away = (dot_nt(d_gate[half:], wg) + dot_nt(d_up[half:], wu)).astype(BF)
    d_gate, d_up = behind([d_gate, d_up], *got_down)
    two_own = dot_nt(d_gate[:half], wg) + dot_nt(d_up[:half], wu)
    d_two = reduce_halves(two_away, two_own)
    part_gate = slabs_of(mm_tn(after(second_rows, two_away, two_own), d_gate).astype(BF))
    grad_down = rest_large(half_sum(part_down, got_down))
    got_gate = half_sent(part_gate, got_down)
    part_up = slabs_of(mm_tn(after(second_rows, part_gate), d_up).astype(BF))

    gain_two_part = jnp.sum(d_two * middle * inv_two, axis=0, keepdims=True)
    d_middle = cotangent.astype(F32) + norm_backward(d_two, middle, inv_two, gain_two)
    back_blocks = tensor_blocks(d_middle.astype(BF))
    back_rows = jnp.concatenate(back_blocks, axis=0)
    got_gate = behind(got_gate, part_up)
    grad_gate = rest_large(half_sum(part_gate, got_gate))
    got_up = half_sent(part_up, got_gate)
    d_head = mm(after(back_rows, *got_gate), wo_t).astype(BF)
    dq, dprev, dkv = attention_backward(blocks, queries, earlier, keyvals, qseg, kseg, d_head, lse, nt)
    later = shift(dprev, "context", -1)
    ffn = reduce_tensor(lambda i, j: dot_nt(after(hidden, dq)[i:j], wd_t), rows)
    output = (middle + ffn).astype(BF)
    part_out = slabs_of(mm_tn(after(back_rows, dq), heads_out).astype(BF))

    dkv = (dkv + later.astype(F32)).astype(BF)
    d_one = reduce_tensor(lambda i, j: dot_nt(dq[i:j], wq) + dot_nt(dkv[i:j], wkv), rows)
    inv_one = rms_inverse(own_in)
    input_grad = d_middle + norm_backward(d_one, own_in, inv_one, gain_one)

    query_part = mm_tn(normed_one, dq)
    kv_part = mm_tn(normed_one, dkv)
    gain_one_part = jnp.sum(query_part * wq.astype(F32), axis=1, keepdims=True) + jnp.sum(kv_part * wkv.astype(F32), axis=1, keepdims=True)
    gain_one_part = gain_one_part / gain_cols[:, 0:1]
    small_part = jnp.concatenate([kv_part, gain_one_part, gain_two_part.T, jnp.zeros((width, 126), F32)], axis=1)
    small_part = small_part.reshape(-1, nt, part, kv_cols + 128)
    small_part = jnp.stack([lax.dynamic_index_in_dim(small_part, t ^ k, 1, False) for k in order])
    small_part = after(small_part, *got_up)
    small_part = reduce_tensor(lambda i, j: small_part[i:j], nt)[0].astype(BF)
    last = jnp.concatenate([slabs_of(query_part.astype(BF)), small_part.reshape(nf, nc, part, kv_cols + 128), part_out], axis=2)
    got_last = half_sent(last, got_up)
    grad_up = rest_large(half_sum(part_up, got_up))
    last, _ = rest_small(half_sum(last, got_last))
    grad_query, small_sum, grad_out = last[: nt * part], last[nt * part : nt * part + part], last[nt * part + part :]
    grad_keyval = small_sum[:, :kv_cols]
    grad_gains = small_sum[:, kv_cols : kv_cols + 2].T
    return (output[None], input_grad[None], grad_query, grad_keyval, grad_out.T, grad_gate, grad_up, grad_down.T, grad_gains)


def solution(mesh):
    rows = P("fsdp", ("context", "tensor"), None)
    column = P(("fsdp", "context"), "tensor")
    row = P("tensor", ("fsdp", "context"))
    small = P(("fsdp", "context", "tensor"), None)
    gains = P(None, ("fsdp", "context", "tensor"))
    return jax.shard_map(
        local,
        mesh=mesh,
        in_specs=(rows, rows, P("fsdp", None), column, small, row, column, column, row, gains),
        out_specs=(rows, rows, column, small, row, column, column, row, gains),
        check_vma=False,
    )
```

```python
import functools

import jax
import jax.numpy as jnp
from jax import lax
from jax.experimental import pallas as pl
from jax.experimental.pallas import tpu as pltpu
from jax.sharding import PartitionSpec as P

HEAD_DIM = 128
WINDOW = 1024
EPSILON = 1e-06
LOG2E = 1.4426950408889634
SCALE = HEAD_DIM**-0.5
BF = jnp.bfloat16
F32 = jnp.float32


def swap(value, axis, k):
    count = lax.axis_size(axis)
    return lax.ppermute(value, axis, [(i, i ^ k) for i in range(count)])


def shift(value, axis, steps):
    count = lax.axis_size(axis)
    leading, last = max(0, -steps), min(count, count - steps)
    return lax.ppermute(value, axis, [(i, i + steps) for i in range(leading, last)])


def bits_of(count):
    return [1 << b for b in range(count.bit_length() - 1)]


def tensor_order(count):
    order = [0]
    for bit in reversed(bits_of(count)):
        order = order + [k ^ bit for k in order]
    return order


def after(value, *deps):
    return lax.optimization_barrier((value,) + deps)[0]


def tensor_blocks(value, first=(), later=()):
    pieces = behind([value], *first)
    bits = list(reversed(bits_of(lax.axis_size("tensor"))))
    for n, bit in enumerate(bits):
        if n == len(bits) - 1 and later:
            pieces = behind(pieces, *later)
        pieces = pieces + [swap(p, "tensor", bit) for p in pieces]
    return pieces


def reduce_halves(away, own):
    bits = bits_of(lax.axis_size("tensor"))
    back = swap(away.astype(BF), "tensor", bits[0])
    total = own + back.astype(F32)
    for bit in bits[1:]:
        half = total.shape[0] // 2
        back = swap(total[half:].astype(BF), "tensor", bit)
        total = total[:half] + back.astype(F32)
    return total


def reduce_tensor(make, rows):
    half = rows // 2
    return reduce_halves(make(half, rows), make(0, half))


def behind(values, *deps):
    return list(lax.optimization_barrier((tuple(values), deps))[0])


def across(value, *deps):
    (value,) = behind([value], *deps)
    return [swap(value, "context", k) for k in range(1, lax.axis_size("context"))]


def along(value, *deps):
    (value,) = behind([value], *deps)
    return [swap(value, "fsdp", k) for k in range(1, lax.axis_size("fsdp"))]


def place_kernel(cuts, slots, *refs):
    n_out = len(cuts)
    ins, outs, sems = refs[: -n_out - 1], refs[-n_out - 1 : -1], refs[-1]
    copies, n = [], 0
    for ref in ins:
        for i in range(ref.shape[0]):
            for out, (first, last) in zip(outs, cuts):
                copies.append(pltpu.make_async_copy(ref.at[i, first:last], out.at[slots[n]], sems.at[len(copies)]))
                copies[-1].start()
            n += 1
    for copy in copies:
        copy.wait()


def place(slots, pieces, cuts=None):
    count = sum(p.shape[0] for p in pieces)
    rows, n = pieces[0].shape[1:]
    cuts = cuts or [(0, rows)]
    anywhere = pl.BlockSpec(memory_space=pl.ANY)
    shapes = [(count, last - first, n) for first, last in cuts]
    out = pl.pallas_call(
        functools.partial(place_kernel, cuts),
        grid_spec=pltpu.PrefetchScalarGridSpec(
            num_scalar_prefetch=1,
            grid=(1,),
            in_specs=[anywhere] * len(pieces),
            out_specs=[whole_spec(shape) for shape in shapes],
            scratch_shapes=[pltpu.SemaphoreType.DMA((count * len(cuts),))],
        ),
        out_shape=[jax.ShapeDtypeStruct(shape, pieces[0].dtype) for shape in shapes],
        cost_estimate=pl.CostEstimate(flops=1, bytes_accessed=1, transcendentals=0),
        name="place",
    )(slots, *pieces)
    return [x.reshape(-1, n) for x in out]


def gathered(own, others, early, later):
    pieces = [own[None], others]
    for e, a in zip(early, later):
        pieces += [e[None], a]
    return pieces


def slots_of():
    nf, nc = lax.axis_size("fsdp"), lax.axis_size("context")
    f, c = lax.axis_index("fsdp"), lax.axis_index("context")
    js = jnp.array([j for _ in range(nc) for j in range(nf)], jnp.int32)
    ks = jnp.array([k for k in range(nc) for _ in range(nf)], jnp.int32)
    return (js ^ f) * nc + (ks ^ c)


def away_half(slabs):
    c = lax.axis_index("context")
    return [lax.dynamic_index_in_dim(slabs, c ^ k, 1, False) for k in range(1, lax.axis_size("context"))]


def half_sent(slabs, *deps):
    sent = behind(away_half(slabs), *deps)
    return [swap(x, "context", k + 1) for k, x in enumerate(sent)]


def half_sum(slabs, got):
    return lax.dynamic_index_in_dim(slabs, lax.axis_index("context"), 1, False).astype(F32) + sum(x.astype(F32) for x in got)


def rest_large(total):
    return lax.psum_scatter(total.astype(BF), "fsdp", scatter_dimension=0, tiled=False).astype(F32)


def rest_small(total, *deps):
    nf, f = lax.axis_size("fsdp"), lax.axis_index("fsdp")
    away = behind([lax.dynamic_index_in_dim(total, f ^ k, 0, False).astype(BF) for k in range(1, nf)], *deps)
    back = [swap(x, "fsdp", k + 1) for k, x in enumerate(away)]
    return lax.dynamic_index_in_dim(total, f, 0, False) + sum(x.astype(F32) for x in back), back


def slabs_of(part):
    nf, nc = lax.axis_size("fsdp"), lax.axis_size("context")
    return part.reshape(nf, nc, part.shape[0] // (nf * nc), part.shape[1])


def dot_nt(a, b):
    return lax.dot_general(a, b, (((1,), (1,)), ((), ())), preferred_element_type=F32)


def dot_nn(a, b):
    return lax.dot_general(a, b, (((1,), (0,)), ((), ())), preferred_element_type=F32)


def in_order(blocks_ref, prev_ref, own_ref, both, count, rows):
    for r in range(count):
        at = blocks_ref[r] * rows
        both[pl.ds(at, rows), :] = prev_ref[r * rows : (r + 1) * rows, :]
        both[pl.ds(at + count * rows, rows), :] = own_ref[r * rows : (r + 1) * rows, :]


def fill_bias(a, rows, count, qseg_ref, kseg_ref, bias, tri):
    qs = qseg_ref[...]
    wide = rows // 128

    def seg(i):
        s = kseg_ref[pl.ds((a + i) * rows, rows), :]
        return jnp.concatenate([s] * wide, axis=1) == qs

    first = (tri & seg(count)) | (jnp.logical_not(tri) & seg(0))
    bias[0] = jnp.where(first, 0.0, -1e30).astype(F32)
    for i in range(1, count):
        bias[i] = jnp.where(seg(i), 0.0, -1e30).astype(F32)


def attend_forward(blocks_ref, q_ref, prev_ref, own_ref, qseg_ref, kseg_ref, out_ref, lse_ref, both, vt, bias):
    count, rows, heads = bias.shape[0], q_ref.shape[0], q_ref.shape[1] // HEAD_DIM
    r = pl.program_id(0)
    a = blocks_ref[r]

    @pl.when(r == 0)
    def _():
        in_order(blocks_ref, prev_ref, own_ref, both, count, rows)
        for i in range(2 * count):
            vt[:, i * rows : (i + 1) * rows] = both[i * rows : (i + 1) * rows, HEAD_DIM:].T

    tri = lax.broadcasted_iota(jnp.int32, (rows, rows), 0) <= lax.broadcasted_iota(jnp.int32, (rows, rows), 1)
    fill_bias(a, rows, count, qseg_ref, kseg_ref, bias, tri)
    starts = [pl.multiple_of((a + i) * rows, rows) for i in range(count + 1)]
    for h in range(heads):
        q = q_ref[:, h * HEAD_DIM : (h + 1) * HEAD_DIM]
        s = [dot_nt(both[pl.ds(st, rows), :HEAD_DIM], q) for st in starts]
        s = [jnp.where(tri, s[count], s[0])] + s[1:count]
        s = [x * (SCALE * LOG2E) + bias[i] for i, x in enumerate(s)]
        top = functools.reduce(jnp.maximum, s)
        top = jnp.max(top, axis=0, keepdims=True)
        p = [jnp.exp2(x - top) for x in s]
        total = jnp.sum(functools.reduce(jnp.add, p), axis=0, keepdims=True)
        low = [x.astype(BF) for x in p]
        zero = jnp.zeros_like(low[0])
        low = [jnp.where(tri, zero, low[0])] + low[1:] + [jnp.where(tri, low[0], zero)]
        acc = None
        for i in range(count + 1):
            d = dot_nn(vt[:, pl.ds(starts[i], rows)], low[i])
            acc = d if acc is None else acc + d
        out_ref[:, h * HEAD_DIM : (h + 1) * HEAD_DIM] = (acc / total).T.astype(BF)
        lse_ref[h : h + 1, :] = top + jnp.log2(total)


def attend_backward(
    blocks_ref, q_ref, prev_ref, own_ref, qseg_ref, kseg_ref, dout_ref, lse_ref, dq_ref, dboth_ref, both, kt, bias, dkv
):
    count, rows, heads = bias.shape[0], q_ref.shape[0], q_ref.shape[1] // HEAD_DIM
    r = pl.program_id(0)
    a = blocks_ref[r]

    @pl.when(r == 0)
    def _():
        in_order(blocks_ref, prev_ref, own_ref, both, count, rows)
        for i in range(2 * count):
            kt[:, i * rows : (i + 1) * rows] = both[i * rows : (i + 1) * rows, :HEAD_DIM].T
        dkv[...] = jnp.zeros_like(dkv)

    tri = lax.broadcasted_iota(jnp.int32, (rows, rows), 0) <= lax.broadcasted_iota(jnp.int32, (rows, rows), 1)
    fill_bias(a, rows, count, qseg_ref, kseg_ref, bias, tri)
    starts = [pl.multiple_of((a + i) * rows, rows) for i in range(count + 1)]
    for h in range(heads):
        cols = slice(h * HEAD_DIM, (h + 1) * HEAD_DIM)
        q, dout = q_ref[:, cols], dout_ref[:, cols]
        lse = lse_ref[h : h + 1, :]
        s = [dot_nt(both[pl.ds(st, rows), :HEAD_DIM], q) for st in starts]
        dp = [dot_nt(both[pl.ds(st, rows), HEAD_DIM:], dout) for st in starts]
        s = [jnp.where(tri, s[count], s[0])] + s[1:count]
        dp = [jnp.where(tri, dp[count], dp[0])] + dp[1:count]
        p = [jnp.exp2(x * (SCALE * LOG2E) + bias[i] - lse) for i, x in enumerate(s)]
        inner = functools.reduce(jnp.add, [x * y for x, y in zip(p, dp)])
        inner = jnp.sum(inner, axis=0, keepdims=True)
        ds = [(x * (y - inner)).astype(BF) for x, y in zip(p, dp)]
        low = [x.astype(BF) for x in p]
        zero = jnp.zeros_like(low[0])
        low = [jnp.where(tri, zero, low[0])] + low[1:] + [jnp.where(tri, low[0], zero)]
        ds = [jnp.where(tri, zero, ds[0])] + ds[1:] + [jnp.where(tri, ds[0], zero)]
        acc = None
        for i in range(count + 1):
            d = dot_nn(kt[:, pl.ds(starts[i], rows)], ds[i])
            acc = d if acc is None else acc + d
            dkv[pl.ds(starts[i], rows), :HEAD_DIM] += dot_nn(ds[i], q)
            dkv[pl.ds(starts[i], rows), HEAD_DIM:] += dot_nn(low[i], dout)
        dq_ref[:, cols] = (acc * SCALE).T.astype(BF)

    @pl.when(r == count - 1)
    def _():
        for j in range(count):
            at = blocks_ref[j] * rows
            for k in range(2):
                blk = dkv[pl.ds(at + k * count * rows, rows), :]
                first = k * 2 * HEAD_DIM
                dboth_ref[j * rows : (j + 1) * rows, first : first + HEAD_DIM] = (blk[:, :HEAD_DIM] * SCALE).astype(BF)
                dboth_ref[j * rows : (j + 1) * rows, first + HEAD_DIM : first + 2 * HEAD_DIM] = blk[:, HEAD_DIM:].astype(BF)


def whole_spec(shape):
    return pl.BlockSpec(shape, lambda r, b: (0,) * len(shape))


def attention_forward(blocks, queries, prev, own, qseg, kseg, count):
    total, width = queries.shape
    rows = total // count
    heads = width // HEAD_DIM
    return pl.pallas_call(
        attend_forward,
        grid_spec=pltpu.PrefetchScalarGridSpec(
            num_scalar_prefetch=1,
            grid=(count,),
            in_specs=[
                pl.BlockSpec((rows, width), lambda r, b: (r, 0)),
                whole_spec(prev.shape),
                whole_spec(own.shape),
                pl.BlockSpec((1, rows), lambda r, b: (0, b[r])),
                whole_spec(kseg.shape),
            ],
            out_specs=[
                pl.BlockSpec((rows, width), lambda r, b: (r, 0)),
                pl.BlockSpec((heads, rows), lambda r, b: (0, r)),
            ],
            scratch_shapes=[
                pltpu.VMEM((2 * total, 2 * HEAD_DIM), BF),
                pltpu.VMEM((HEAD_DIM, 2 * total), BF),
                pltpu.VMEM((count, rows, rows), F32),
            ],
        ),
        out_shape=[jax.ShapeDtypeStruct((total, width), BF), jax.ShapeDtypeStruct((heads, total), F32)],
        compiler_params=pltpu.CompilerParams(vmem_limit_bytes=40 << 20),
        cost_estimate=pl.CostEstimate(flops=1, bytes_accessed=1, transcendentals=0),
        name="attend_forward",
    )(blocks, queries, prev, own, qseg, kseg)


def attention_backward(blocks, queries, prev, own, qseg, kseg, dout, lse, count):
    total, width = queries.shape
    rows = total // count
    heads = width // HEAD_DIM
    return pl.pallas_call(
        attend_backward,
        grid_spec=pltpu.PrefetchScalarGridSpec(
            num_scalar_prefetch=1,
            grid=(count,),
            in_specs=[
                pl.BlockSpec((rows, width), lambda r, b: (r, 0)),
                whole_spec(prev.shape),
                whole_spec(own.shape),
                pl.BlockSpec((1, rows), lambda r, b: (0, b[r])),
                whole_spec(kseg.shape),
                pl.BlockSpec((rows, width), lambda r, b: (r, 0)),
                pl.BlockSpec((heads, rows), lambda r, b: (0, r)),
            ],
            out_specs=[
                pl.BlockSpec((rows, width), lambda r, b: (r, 0)),
                whole_spec((total, 4 * HEAD_DIM)),
            ],
            scratch_shapes=[
                pltpu.VMEM((2 * total, 2 * HEAD_DIM), BF),
                pltpu.VMEM((HEAD_DIM, 2 * total), BF),
                pltpu.VMEM((count, rows, rows), F32),
                pltpu.VMEM((2 * total, 2 * HEAD_DIM), F32),
            ],
        ),
        out_shape=[
            jax.ShapeDtypeStruct((total, width), BF),
            jax.ShapeDtypeStruct((total, 4 * HEAD_DIM), BF),
        ],
        compiler_params=pltpu.CompilerParams(vmem_limit_bytes=40 << 20),
        cost_estimate=pl.CostEstimate(flops=1, bytes_accessed=1, transcendentals=0),
        name="attend_backward",
    )(blocks, queries, prev, own, qseg, kseg, dout, lse)


def gelu_parts(g):
    root = 0.7978845608028654
    inner = jnp.tanh(root * (g + 0.044715 * (g * g * g)))
    half = 0.5 * (1.0 + inner)
    slope = half + 0.5 * g * (1.0 - inner * inner) * (root * (1.0 + 3 * 0.044715 * (g * g)))
    return g * half, slope


def ffn_forward_kernel(nx, *refs):
    xs, cs, (gate, up) = refs[:nx], refs[nx : 2 * nx], refs[2 * nx : 2 * nx + 2]
    hid, act, pg, x_out, c_out, x_all, c_all, sems, o_sems = refs[2 * nx + 2 :]
    rows, n = xs[0].shape[0], gate.shape[1]
    i = pl.program_id(0)
    x_in = [pltpu.make_async_copy(x, x_all.at[pl.ds(j * rows, rows)], sems.at[j]) for j, x in enumerate(xs)]
    c_in = [pltpu.make_async_copy(x, c_all.at[pl.ds(j * rows, rows)], sems.at[nx + j]) for j, x in enumerate(cs)]
    outs = [pltpu.make_async_copy(src, dst, o_sems.at[j]) for j, (src, dst) in enumerate(((x_all, x_out), (c_all, c_out)))]

    @pl.when(i == 0)
    def _():
        for copy in x_in + c_in:
            copy.start()
        for copy in x_in:
            copy.wait()
        outs[0].start()

    @pl.when(i == 1)
    def _():
        for copy in c_in:
            copy.wait()
        outs[1].start()

    x = x_all[pl.ds(pl.multiple_of(i * rows, rows), rows), :]
    step = n // 3 if n % 384 == 0 else n
    for j in range(0, n, step):
        g = dot_nn(x, gate[:, j : j + step])
        u = dot_nn(x, up[:, j : j + step])
        value, slope = gelu_parts(g)
        hid[:, j : j + step] = (value * u).astype(BF)
        act[:, j : j + step] = value.astype(BF)
        pg[:, j : j + step] = (slope * u).astype(BF)

    @pl.when(i == pl.num_programs(0) - 1)
    def _():
        for o in outs:
            o.wait()


def ffn_forward(x_blocks, c_blocks, both):
    rows, width = x_blocks[0].shape
    count, n = len(x_blocks), both.shape[1] // 3
    total = count * rows
    anywhere = pl.BlockSpec(memory_space=pl.ANY)
    block = pl.BlockSpec((rows, n), lambda i: (i, 0))
    kept = jax.ShapeDtypeStruct((total, n), BF)
    return pl.pallas_call(
        functools.partial(ffn_forward_kernel, count),
        grid=(count,),
        in_specs=[anywhere] * (2 * count) + [pl.BlockSpec((width, n), lambda i: (0, 0)), pl.BlockSpec((width, n), lambda i: (0, 1))],
        out_specs=[block] * 3 + [anywhere] * 2,
        scratch_shapes=[
            pltpu.VMEM((total, width), BF),
            pltpu.VMEM((total, width), BF),
            pltpu.SemaphoreType.DMA((2 * count,)),
            pltpu.SemaphoreType.DMA((2,)),
        ],
        out_shape=[kept] * 3 + [jax.ShapeDtypeStruct((total, width), BF)] * 2,
        compiler_params=pltpu.CompilerParams(vmem_limit_bytes=48 << 20),
        cost_estimate=pl.CostEstimate(flops=4 * total * width * n, bytes_accessed=20 << 20, transcendentals=total * n),
        name="ffn_forward",
    )(*x_blocks, *c_blocks, both, both)


def ffn_backward_kernel(cot, act, pg, down, grads):
    n = down.shape[1]
    x = cot[...]
    step = n // 3 if n % 384 == 0 else n
    for j in range(0, n, step):
        d = dot_nn(x, down[:, j : j + step])
        grads[:, j : j + step] = (d * pg[:, j : j + step].astype(F32)).astype(BF)
        grads[:, n + j : n + j + step] = (d * act[:, j : j + step].astype(F32)).astype(BF)


def ffn_backward(cot, act, pg, down, count):
    total, width = cot.shape
    n = down.shape[1] // 3
    rows = total // count
    block = pl.BlockSpec((rows, n), lambda i: (i, 0))
    return pl.pallas_call(
        ffn_backward_kernel,
        grid=(count,),
        in_specs=[pl.BlockSpec((rows, width), lambda i: (i, 0)), block, block, pl.BlockSpec((width, n), lambda i: (0, 2))],
        out_specs=pl.BlockSpec((rows, 2 * n), lambda i: (i, 0)),
        out_shape=jax.ShapeDtypeStruct((total, 2 * n), BF),
        compiler_params=pltpu.CompilerParams(vmem_limit_bytes=40 << 20),
        cost_estimate=pl.CostEstimate(flops=2 * total * width * n, bytes_accessed=16 << 20, transcendentals=0),
        name="ffn_backward",
    )(cot, act, pg, down)


def rms_inverse(values):
    return lax.rsqrt(jnp.mean(values * values, axis=-1, keepdims=True) + EPSILON)


def norm_backward(grad_normed, values, inv_rms, gain_row):
    scaled = grad_normed * gain_row
    inner_sum = jnp.mean(scaled * values, axis=-1, keepdims=True)
    return inv_rms * scaled - values * (inv_rms * inv_rms * inv_rms) * inner_sum


def mm(a, b):
    return dot_nn(a, b)


def mm_tn(a, b):
    return lax.dot_general(a, b, (((0,), (0,)), ((), ())), preferred_element_type=F32)


def local(tokens, cotangent, segment_ids, w_query, w_keyval, w_out, w_gate, w_up, w_down, norm_gains):
    nt = lax.axis_size("tensor")
    t, c = lax.axis_index("tensor"), lax.axis_index("context")
    tokens, cotangent = tokens[0], cotangent[0]
    own_rows, width = tokens.shape
    rows = own_rows * nt
    if rows != WINDOW:
        raise ValueError("shard length")
    order = tensor_order(nt)
    blocks = jnp.array(order, jnp.int32) ^ t

    part = w_keyval.shape[0]
    kv_cols = w_keyval.shape[1]
    nf, nc = lax.axis_size("fsdp"), lax.axis_size("context")
    small_own = jnp.concatenate([w_keyval, norm_gains.T, jnp.zeros((part, 126), BF)], axis=1)
    first_own = jnp.concatenate([w_query, small_own], axis=0)
    wo_own, wd_own = w_out.T, w_down.T
    slots = slots_of()
    both = ("fsdp", "context")

    first_along = along(first_own)
    first_early = across(first_own)
    token_blocks = tensor_blocks(tokens)
    first_along = along(first_own)
    first_early = across(first_own)
    token_blocks = tensor_blocks(tokens)
    wg = lax.all_gather(w_gate, both, axis=0, tiled=True)
    first_along = jnp.stack(first_along)
    first_across = across(first_along, first_early)
    gate_up = jnp.concatenate([w_gate, w_up, wd_own], axis=1)
    gate_up = lax.all_gather(after(gate_up, *first_along), both, axis=0, tiled=True)
    first_along = jnp.stack(first_along)
    first_across = across(first_along, first_early)
    wu = lax.all_gather(after(w_up, *first_across), both, axis=0, tiled=True)
    wo_along = along(wo_own, first_along)
    wo_all = jnp.stack([wo_own, *wo_along])
    wo_across = across(wo_all, first_across)

    own_rows_q = nt * part
    wq, small = place(slots, gathered(first_own, first_along, first_early, first_across), [(0, own_rows_q), (own_rows_q, own_rows_q + part)])
    small_blocks = tensor_blocks(small.reshape(nf * nc, part, -1))
    cot_blocks = tensor_blocks(cotangent, small_blocks)
    small = jnp.zeros((nf * nc, nt, part, small.shape[1]), BF)
    for i in range(nt):
        small = lax.dynamic_update_index_in_dim(small, small_blocks[i], t ^ order[i], 1)
    small = small.reshape(width, -1)
    wkv = small[:, :kv_cols]
    gain_cols = small[:, kv_cols : kv_cols + 2].astype(F32)
    gains = gain_cols.T
    gain_one, gain_two = gains[0:1], gains[1:2]

    ids = segment_ids[0]
    own_seg = lax.dynamic_slice_in_dim(ids, c * rows, rows, 0)
    prev_seg = lax.dynamic_slice_in_dim(ids, jnp.maximum(c - 1, 0) * rows, rows, 0)
    prev_seg = jnp.where(c > 0, prev_seg, -1)
    qseg = own_seg[None, :]
    kseg = jnp.broadcast_to(jnp.concatenate([prev_seg, own_seg])[:, None], (2 * rows, 128))

    xin = jnp.concatenate(token_blocks, axis=0).astype(F32)
    inv_one_rows = rms_inverse(xin)
    normed_one = (xin * inv_one_rows * gain_one).astype(BF)
    keyvals = mm(normed_one, wkv).astype(BF)
    earlier = shift(keyvals, "context", 1)
    queries = mm(normed_one, wq).astype(BF)
    heads_out, lse = attention_forward(blocks, after(queries, cot_blocks[1]), earlier, keyvals, qseg, kseg, nt)
    (wo_t,) = place(slots, [wo_all] + behind(wo_across, heads_out))
    heads_now = heads_out
    branch = reduce_tensor(lambda i, j: dot_nt(heads_now[i:j], wo_t), rows)
    own_in = tokens.astype(F32)
    middle = own_in + branch
    inv_two = rms_inverse(middle)
    normed_two = (middle * inv_two * gain_two).astype(BF)
    second_blocks = tensor_blocks(normed_two)

    hidden, act, pg, second_rows, cot_rows = ffn_forward(second_blocks, cot_blocks, gate_up)
    part_down = slabs_of(mm_tn(cot_rows, hidden).astype(BF))
    got_down = half_sent(part_down)
    grads = ffn_backward(after(cot_rows, part_down), act, pg, gate_up, nt)
    ff = w_gate.shape[1]
    gate_up, wd_t = gate_up[:, : 2 * ff], gate_up[:, 2 * ff :]
    half = rows // 2
    two_away = dot_nt(grads[half:], gate_up).astype(BF)
    two_own = dot_nt(grads[:half], gate_up)
    d_two = reduce_halves(two_away, two_own)
    part_gate = slabs_of(mm_tn(after(second_rows, two_away, two_own), grads[:, :ff]).astype(BF))
    got_down = behind(got_down, part_gate)
    grad_down = rest_large(half_sum(part_down, got_down))
    got_gate = half_sent(part_gate, got_down)
    part_up = slabs_of(mm_tn(after(second_rows, part_gate), grads[:, ff:]).astype(BF))

    gain_two_part = jnp.sum(d_two * middle * inv_two, axis=0, keepdims=True)
    d_middle = cotangent.astype(F32) + norm_backward(d_two, middle, inv_two, gain_two)
    back_blocks = tensor_blocks(d_middle.astype(BF))
    hidden = after(hidden, back_blocks[1])
    ffn = reduce_tensor(lambda i, j: dot_nt(hidden[i:j], wd_t), rows)
    output = (middle + ffn).astype(BF)
    back_rows = jnp.concatenate(back_blocks, axis=0)
    got_gate = behind(got_gate, part_up)
    grad_gate = rest_large(half_sum(part_gate, got_gate))
    got_up = half_sent(part_up, got_gate)
    d_head = mm(after(back_rows, *got_gate), wo_t).astype(BF)
    dq, dboth = attention_backward(blocks, queries, earlier, keyvals, qseg, kseg, d_head, lse, nt)
    dboth = reduce_halves(dboth[rows // 2 :], dboth[: rows // 2].astype(F32))
    later = shift(dboth[:, :kv_cols].astype(BF), "context", -1)
    dkv = (dboth[:, kv_cols:] + later.astype(F32)).astype(BF)
    got_up = behind(got_up, dq)
    part_out = slabs_of(mm_tn(after(back_rows, dq), heads_out).astype(BF))

    d_one = reduce_tensor(lambda i, j: dot_nt(dq[i:j], wq), rows) + dot_nt(dkv, wkv)
    inv_one = rms_inverse(own_in)
    input_grad = d_middle + norm_backward(d_one, own_in, inv_one, gain_one)

    query_part = mm_tn(normed_one, dq)
    kv_part = mm_tn(normed_one[:own_rows], dkv)
    gain_one_part = jnp.sum(query_part * wq.astype(F32), axis=1, keepdims=True) + jnp.sum(kv_part * wkv.astype(F32), axis=1, keepdims=True)
    gain_one_part = gain_one_part / gain_cols[:, 0:1]
    small_part = jnp.concatenate([kv_part, gain_one_part, gain_two_part.T, jnp.zeros((width, 126), F32)], axis=1)
    small_part = small_part.reshape(-1, nt, part, kv_cols + 128)
    small_part = jnp.stack([lax.dynamic_index_in_dim(small_part, t ^ k, 1, False) for k in order])
    small_part = after(small_part, *got_up)
    small_part = reduce_tensor(lambda i, j: small_part[i:j], nt)[0].astype(BF)
    last = jnp.concatenate([slabs_of(query_part.astype(BF)), part_out], axis=2)
    got_last = half_sent(last, got_up)
    grad_up = rest_large(half_sum(part_up, got_up))
    small_part = small_part.reshape(nf, nc, part, kv_cols + 128)
    got_small = half_sent(small_part)
    small_sum, back = rest_small(half_sum(small_part, got_small))
    last, _ = rest_small(half_sum(last, got_last), back)
    grad_query, grad_out = last[: nt * part], last[nt * part :]
    grad_keyval = small_sum[:, :kv_cols]
    grad_gains = small_sum[:, kv_cols : kv_cols + 2].T
    return (output[None], input_grad[None], grad_query, grad_keyval, grad_out.T, grad_gate, grad_up, grad_down.T, grad_gains)


def solution(mesh):
    rows = P("fsdp", ("context", "tensor"), None)
    column = P(("fsdp", "context"), "tensor")
    row = P("tensor", ("fsdp", "context"))
    small = P(("fsdp", "context", "tensor"), None)
    gains = P(None, ("fsdp", "context", "tensor"))
    return jax.shard_map(
        local,
        mesh=mesh,
        in_specs=(rows, rows, P("fsdp", None), column, small, row, column, column, row, gains),
        out_specs=(rows, rows, column, small, row, column, column, row, gains),
        check_vma=False,
    )
```

```python
import functools

import jax
import jax.numpy as jnp
from jax import lax
from jax.experimental import pallas as pl
from jax.experimental.pallas import tpu as pltpu
from jax.sharding import PartitionSpec as P

HEAD_DIM = 128
WINDOW = 1024
EPSILON = 1e-06
LOG2E = 1.4426950408889634
SCALE = HEAD_DIM**-0.5
BF = jnp.bfloat16
F32 = jnp.float32


def swap(value, axis, k):
    count = lax.axis_size(axis)
    return lax.ppermute(value, axis, [(i, i ^ k) for i in range(count)])


def shift(value, axis, steps):
    count = lax.axis_size(axis)
    leading, last = max(0, -steps), min(count, count - steps)
    return lax.ppermute(value, axis, [(i, i + steps) for i in range(leading, last)])


def bits_of(count):
    return [1 << b for b in range(count.bit_length() - 1)]


def tensor_order(count):
    order = [0]
    for bit in reversed(bits_of(count)):
        order = order + [k ^ bit for k in order]
    return order


def after(value, *deps):
    return lax.optimization_barrier((value,) + deps)[0]


def tensor_blocks(value, first=(), later=()):
    pieces = behind([value], *first)
    bits = list(reversed(bits_of(lax.axis_size("tensor"))))
    for n, bit in enumerate(bits):
        if n == len(bits) - 1 and later:
            pieces = behind(pieces, *later)
        pieces = pieces + [swap(p, "tensor", bit) for p in pieces]
    return pieces


def reduce_halves(away, own):
    bits = bits_of(lax.axis_size("tensor"))
    back = swap(away.astype(BF), "tensor", bits[0])
    total = own + back.astype(F32)
    for bit in bits[1:]:
        half = total.shape[0] // 2
        back = swap(total[half:].astype(BF), "tensor", bit)
        total = total[:half] + back.astype(F32)
    return total


def reduce_tensor(make, rows):
    half = rows // 2
    return reduce_halves(make(half, rows), make(0, half))


def behind(values, *deps):
    return list(lax.optimization_barrier((tuple(values), deps))[0])


def across(value, *deps):
    (value,) = behind([value], *deps)
    return [swap(value, "context", k) for k in range(1, lax.axis_size("context"))]


def along(value, *deps):
    (value,) = behind([value], *deps)
    return [swap(value, "fsdp", k) for k in range(1, lax.axis_size("fsdp"))]


def place_kernel(cuts, slots, *refs):
    n_out = len(cuts)
    ins, outs, sems = refs[: -n_out - 1], refs[-n_out - 1 : -1], refs[-1]
    copies, n = [], 0
    for ref in ins:
        for i in range(ref.shape[0]):
            for out, (first, last) in zip(outs, cuts):
                copies.append(pltpu.make_async_copy(ref.at[i, first:last], out.at[slots[n]], sems.at[len(copies)]))
                copies[-1].start()
            n += 1
    for copy in copies:
        copy.wait()


def place(slots, pieces, cuts=None):
    count = sum(p.shape[0] for p in pieces)
    rows, n = pieces[0].shape[1:]
    cuts = cuts or [(0, rows)]
    anywhere = pl.BlockSpec(memory_space=pl.ANY)
    shapes = [(count, last - first, n) for first, last in cuts]
    out = pl.pallas_call(
        functools.partial(place_kernel, cuts),
        grid_spec=pltpu.PrefetchScalarGridSpec(
            num_scalar_prefetch=1,
            grid=(1,),
            in_specs=[anywhere] * len(pieces),
            out_specs=[whole_spec(shape) for shape in shapes],
            scratch_shapes=[pltpu.SemaphoreType.DMA((count * len(cuts),))],
        ),
        out_shape=[jax.ShapeDtypeStruct(shape, pieces[0].dtype) for shape in shapes],
        cost_estimate=pl.CostEstimate(flops=1, bytes_accessed=1, transcendentals=0),
        name="place",
    )(slots, *pieces)
    return [x.reshape(-1, n) for x in out]


def gathered(own, others, early, later):
    pieces = [own[None], others]
    for e, a in zip(early, later):
        pieces += [e[None], a]
    return pieces


def slots_of():
    nf, nc = lax.axis_size("fsdp"), lax.axis_size("context")
    f, c = lax.axis_index("fsdp"), lax.axis_index("context")
    js = jnp.array([j for _ in range(nc) for j in range(nf)], jnp.int32)
    ks = jnp.array([k for k in range(nc) for _ in range(nf)], jnp.int32)
    return (js ^ f) * nc + (ks ^ c)


def away_half(slabs):
    c = lax.axis_index("context")
    return [lax.dynamic_index_in_dim(slabs, c ^ k, 1, False) for k in range(1, lax.axis_size("context"))]


def half_sent(slabs, *deps):
    sent = behind(away_half(slabs), *deps)
    return [swap(x, "context", k + 1) for k, x in enumerate(sent)]


def half_sum(slabs, got):
    return lax.dynamic_index_in_dim(slabs, lax.axis_index("context"), 1, False).astype(F32) + sum(x.astype(F32) for x in got)


def rest_large(total):
    return lax.psum_scatter(total.astype(BF), "fsdp", scatter_dimension=0, tiled=False).astype(F32)


def rest_small(total, *deps):
    nf, f = lax.axis_size("fsdp"), lax.axis_index("fsdp")
    away = behind([lax.dynamic_index_in_dim(total, f ^ k, 0, False).astype(BF) for k in range(1, nf)], *deps)
    back = [swap(x, "fsdp", k + 1) for k, x in enumerate(away)]
    return lax.dynamic_index_in_dim(total, f, 0, False) + sum(x.astype(F32) for x in back), back


def slabs_of(part):
    nf, nc = lax.axis_size("fsdp"), lax.axis_size("context")
    return part.reshape(nf, nc, part.shape[0] // (nf * nc), part.shape[1])


def dot_nt(a, b):
    return lax.dot_general(a, b, (((1,), (1,)), ((), ())), preferred_element_type=F32)


def dot_nn(a, b):
    return lax.dot_general(a, b, (((1,), (0,)), ((), ())), preferred_element_type=F32)


def in_order(blocks_ref, prev_ref, own_ref, both, count, rows):
    for r in range(count):
        at = blocks_ref[r] * rows
        both[pl.ds(at, rows), :] = prev_ref[r * rows : (r + 1) * rows, :]
        both[pl.ds(at + count * rows, rows), :] = own_ref[r * rows : (r + 1) * rows, :]


def fill_bias(a, rows, count, qseg_ref, kseg_ref, bias, tri):
    qs = qseg_ref[...]
    wide = rows // 128

    def seg(i):
        s = kseg_ref[pl.ds((a + i) * rows, rows), :]
        return jnp.concatenate([s] * wide, axis=1) == qs

    first = (tri & seg(count)) | (jnp.logical_not(tri) & seg(0))
    bias[0] = jnp.where(first, 0.0, -1e30).astype(F32)
    for i in range(1, count):
        bias[i] = jnp.where(seg(i), 0.0, -1e30).astype(F32)


def attend_forward(blocks_ref, q_ref, prev_ref, own_ref, qseg_ref, kseg_ref, out_ref, lse_ref, both, vt, bias):
    count, rows, heads = bias.shape[0], q_ref.shape[0], q_ref.shape[1] // HEAD_DIM
    r = pl.program_id(0)
    a = blocks_ref[r]

    @pl.when(r == 0)
    def _():
        in_order(blocks_ref, prev_ref, own_ref, both, count, rows)
        for i in range(2 * count):
            vt[:, i * rows : (i + 1) * rows] = both[i * rows : (i + 1) * rows, HEAD_DIM:].T

    tri = lax.broadcasted_iota(jnp.int32, (rows, rows), 0) <= lax.broadcasted_iota(jnp.int32, (rows, rows), 1)
    fill_bias(a, rows, count, qseg_ref, kseg_ref, bias, tri)
    starts = [pl.multiple_of((a + i) * rows, rows) for i in range(count + 1)]
    for h in range(heads):
        q = q_ref[:, h * HEAD_DIM : (h + 1) * HEAD_DIM]
        s = [dot_nt(both[pl.ds(st, rows), :HEAD_DIM], q) for st in starts]
        s = [jnp.where(tri, s[count], s[0])] + s[1:count]
        s = [x * (SCALE * LOG2E) + bias[i] for i, x in enumerate(s)]
        top = functools.reduce(jnp.maximum, s)
        top = jnp.max(top, axis=0, keepdims=True)
        p = [jnp.exp2(x - top) for x in s]
        total = jnp.sum(functools.reduce(jnp.add, p), axis=0, keepdims=True)
        low = [x.astype(BF) for x in p]
        zero = jnp.zeros_like(low[0])
        low = [jnp.where(tri, zero, low[0])] + low[1:] + [jnp.where(tri, low[0], zero)]
        acc = None
        for i in range(count + 1):
            d = dot_nn(vt[:, pl.ds(starts[i], rows)], low[i])
            acc = d if acc is None else acc + d
        out_ref[:, h * HEAD_DIM : (h + 1) * HEAD_DIM] = (acc / total).T.astype(BF)
        lse_ref[h : h + 1, :] = top + jnp.log2(total)


def attend_backward(
    blocks_ref, q_ref, prev_ref, own_ref, qseg_ref, kseg_ref, dout_ref, lse_ref, dq_ref, dboth_ref, both, kt, bias, dkv
):
    count, rows, heads = bias.shape[0], q_ref.shape[0], q_ref.shape[1] // HEAD_DIM
    r = pl.program_id(0)
    a = blocks_ref[r]

    @pl.when(r == 0)
    def _():
        in_order(blocks_ref, prev_ref, own_ref, both, count, rows)
        for i in range(2 * count):
            kt[:, i * rows : (i + 1) * rows] = both[i * rows : (i + 1) * rows, :HEAD_DIM].T
        dkv[...] = jnp.zeros_like(dkv)

    tri = lax.broadcasted_iota(jnp.int32, (rows, rows), 0) <= lax.broadcasted_iota(jnp.int32, (rows, rows), 1)
    fill_bias(a, rows, count, qseg_ref, kseg_ref, bias, tri)
    starts = [pl.multiple_of((a + i) * rows, rows) for i in range(count + 1)]
    for h in range(heads):
        cols = slice(h * HEAD_DIM, (h + 1) * HEAD_DIM)
        q, dout = q_ref[:, cols], dout_ref[:, cols]
        lse = lse_ref[h : h + 1, :]
        s = [dot_nt(both[pl.ds(st, rows), :HEAD_DIM], q) for st in starts]
        dp = [dot_nt(both[pl.ds(st, rows), HEAD_DIM:], dout) for st in starts]
        s = [jnp.where(tri, s[count], s[0])] + s[1:count]
        dp = [jnp.where(tri, dp[count], dp[0])] + dp[1:count]
        p = [jnp.exp2(x * (SCALE * LOG2E) + bias[i] - lse) for i, x in enumerate(s)]
        inner = functools.reduce(jnp.add, [x * y for x, y in zip(p, dp)])
        inner = jnp.sum(inner, axis=0, keepdims=True)
        ds = [(x * (y - inner)).astype(BF) for x, y in zip(p, dp)]
        low = [x.astype(BF) for x in p]
        zero = jnp.zeros_like(low[0])
        low = [jnp.where(tri, zero, low[0])] + low[1:] + [jnp.where(tri, low[0], zero)]
        ds = [jnp.where(tri, zero, ds[0])] + ds[1:] + [jnp.where(tri, ds[0], zero)]
        acc = None
        for i in range(count + 1):
            d = dot_nn(kt[:, pl.ds(starts[i], rows)], ds[i])
            acc = d if acc is None else acc + d
            dkv[pl.ds(starts[i], rows), :HEAD_DIM] += dot_nn(ds[i], q)
            dkv[pl.ds(starts[i], rows), HEAD_DIM:] += dot_nn(low[i], dout)
        dq_ref[:, cols] = (acc * SCALE).T.astype(BF)

    @pl.when(r == count - 1)
    def _():
        for j in range(count):
            at = blocks_ref[j] * rows
            for k in range(2):
                blk = dkv[pl.ds(at + k * count * rows, rows), :]
                first = k * 2 * HEAD_DIM
                dboth_ref[j * rows : (j + 1) * rows, first : first + HEAD_DIM] = (blk[:, :HEAD_DIM] * SCALE).astype(BF)
                dboth_ref[j * rows : (j + 1) * rows, first + HEAD_DIM : first + 2 * HEAD_DIM] = blk[:, HEAD_DIM:].astype(BF)


def whole_spec(shape):
    return pl.BlockSpec(shape, lambda r, b: (0,) * len(shape))


def attention_forward(blocks, queries, prev, own, qseg, kseg, count):
    total, width = queries.shape
    rows = total // count
    heads = width // HEAD_DIM
    return pl.pallas_call(
        attend_forward,
        grid_spec=pltpu.PrefetchScalarGridSpec(
            num_scalar_prefetch=1,
            grid=(count,),
            in_specs=[
                pl.BlockSpec((rows, width), lambda r, b: (r, 0)),
                whole_spec(prev.shape),
                whole_spec(own.shape),
                pl.BlockSpec((1, rows), lambda r, b: (0, b[r])),
                whole_spec(kseg.shape),
            ],
            out_specs=[
                pl.BlockSpec((rows, width), lambda r, b: (r, 0)),
                pl.BlockSpec((heads, rows), lambda r, b: (0, r)),
            ],
            scratch_shapes=[
                pltpu.VMEM((2 * total, 2 * HEAD_DIM), BF),
                pltpu.VMEM((HEAD_DIM, 2 * total), BF),
                pltpu.VMEM((count, rows, rows), F32),
            ],
        ),
        out_shape=[jax.ShapeDtypeStruct((total, width), BF), jax.ShapeDtypeStruct((heads, total), F32)],
        compiler_params=pltpu.CompilerParams(vmem_limit_bytes=40 << 20),
        cost_estimate=pl.CostEstimate(flops=1, bytes_accessed=1, transcendentals=0),
        name="attend_forward",
    )(blocks, queries, prev, own, qseg, kseg)


def attention_backward(blocks, queries, prev, own, qseg, kseg, dout, lse, count):
    total, width = queries.shape
    rows = total // count
    heads = width // HEAD_DIM
    return pl.pallas_call(
        attend_backward,
        grid_spec=pltpu.PrefetchScalarGridSpec(
            num_scalar_prefetch=1,
            grid=(count,),
            in_specs=[
                pl.BlockSpec((rows, width), lambda r, b: (r, 0)),
                whole_spec(prev.shape),
                whole_spec(own.shape),
                pl.BlockSpec((1, rows), lambda r, b: (0, b[r])),
                whole_spec(kseg.shape),
                pl.BlockSpec((rows, width), lambda r, b: (r, 0)),
                pl.BlockSpec((heads, rows), lambda r, b: (0, r)),
            ],
            out_specs=[
                pl.BlockSpec((rows, width), lambda r, b: (r, 0)),
                whole_spec((total, 4 * HEAD_DIM)),
            ],
            scratch_shapes=[
                pltpu.VMEM((2 * total, 2 * HEAD_DIM), BF),
                pltpu.VMEM((HEAD_DIM, 2 * total), BF),
                pltpu.VMEM((count, rows, rows), F32),
                pltpu.VMEM((2 * total, 2 * HEAD_DIM), F32),
            ],
        ),
        out_shape=[
            jax.ShapeDtypeStruct((total, width), BF),
            jax.ShapeDtypeStruct((total, 4 * HEAD_DIM), BF),
        ],
        compiler_params=pltpu.CompilerParams(vmem_limit_bytes=40 << 20),
        cost_estimate=pl.CostEstimate(flops=1, bytes_accessed=1, transcendentals=0),
        name="attend_backward",
    )(blocks, queries, prev, own, qseg, kseg, dout, lse)


def gelu_parts(g):
    root = 0.7978845608028654
    inner = jnp.tanh(root * (g + 0.044715 * (g * g * g)))
    half = 0.5 * (1.0 + inner)
    slope = half + 0.5 * g * (1.0 - inner * inner) * (root * (1.0 + 3 * 0.044715 * (g * g)))
    return g * half, slope


def ffn_forward_kernel(nx, *refs):
    xs, cs, (gate, up) = refs[:nx], refs[nx : 2 * nx], refs[2 * nx : 2 * nx + 2]
    hid, act, pg, x_out, c_out, x_all, c_all, sems, o_sems = refs[2 * nx + 2 :]
    rows, n = xs[0].shape[0], gate.shape[1]
    i = pl.program_id(0)
    x_in = [pltpu.make_async_copy(x, x_all.at[pl.ds(j * rows, rows)], sems.at[j]) for j, x in enumerate(xs)]
    c_in = [pltpu.make_async_copy(x, c_all.at[pl.ds(j * rows, rows)], sems.at[nx + j]) for j, x in enumerate(cs)]
    outs = [pltpu.make_async_copy(src, dst, o_sems.at[j]) for j, (src, dst) in enumerate(((x_all, x_out), (c_all, c_out)))]

    @pl.when(i == 0)
    def _():
        for copy in x_in + c_in:
            copy.start()
        for copy in x_in:
            copy.wait()
        outs[0].start()

    @pl.when(i == 1)
    def _():
        for copy in c_in:
            copy.wait()
        outs[1].start()

    x = x_all[pl.ds(pl.multiple_of(i * rows, rows), rows), :]
    step = n // 3 if n % 384 == 0 else n
    for j in range(0, n, step):
        g = dot_nn(x, gate[:, j : j + step])
        u = dot_nn(x, up[:, j : j + step])
        value, slope = gelu_parts(g)
        hid[:, j : j + step] = (value * u).astype(BF)
        act[:, j : j + step] = value.astype(BF)
        pg[:, j : j + step] = (slope * u).astype(BF)

    @pl.when(i == pl.num_programs(0) - 1)
    def _():
        for o in outs:
            o.wait()


def ffn_forward(x_blocks, c_blocks, both):
    rows, width = x_blocks[0].shape
    count, n = len(x_blocks), both.shape[1] // 3
    total = count * rows
    anywhere = pl.BlockSpec(memory_space=pl.ANY)
    block = pl.BlockSpec((rows, n), lambda i: (i, 0))
    kept = jax.ShapeDtypeStruct((total, n), BF)
    return pl.pallas_call(
        functools.partial(ffn_forward_kernel, count),
        grid=(count,),
        in_specs=[anywhere] * (2 * count) + [pl.BlockSpec((width, n), lambda i: (0, 0)), pl.BlockSpec((width, n), lambda i: (0, 1))],
        out_specs=[block] * 3 + [anywhere] * 2,
        scratch_shapes=[
            pltpu.VMEM((total, width), BF),
            pltpu.VMEM((total, width), BF),
            pltpu.SemaphoreType.DMA((2 * count,)),
            pltpu.SemaphoreType.DMA((2,)),
        ],
        out_shape=[kept] * 3 + [jax.ShapeDtypeStruct((total, width), BF)] * 2,
        compiler_params=pltpu.CompilerParams(vmem_limit_bytes=48 << 20),
        cost_estimate=pl.CostEstimate(flops=4 * total * width * n, bytes_accessed=20 << 20, transcendentals=total * n),
        name="ffn_forward",
    )(*x_blocks, *c_blocks, both, both)


def ffn_backward_kernel(cot, act, pg, down, grads):
    n = down.shape[1]
    x = cot[...]
    step = n // 3 if n % 384 == 0 else n
    for j in range(0, n, step):
        d = dot_nn(x, down[:, j : j + step])
        grads[:, j : j + step] = (d * pg[:, j : j + step].astype(F32)).astype(BF)
        grads[:, n + j : n + j + step] = (d * act[:, j : j + step].astype(F32)).astype(BF)


def ffn_backward(cot, act, pg, down, count):
    total, width = cot.shape
    n = down.shape[1] // 3
    rows = total // count
    block = pl.BlockSpec((rows, n), lambda i: (i, 0))
    return pl.pallas_call(
        ffn_backward_kernel,
        grid=(count,),
        in_specs=[pl.BlockSpec((rows, width), lambda i: (i, 0)), block, block, pl.BlockSpec((width, n), lambda i: (0, 2))],
        out_specs=pl.BlockSpec((rows, 2 * n), lambda i: (i, 0)),
        out_shape=jax.ShapeDtypeStruct((total, 2 * n), BF),
        compiler_params=pltpu.CompilerParams(vmem_limit_bytes=40 << 20),
        cost_estimate=pl.CostEstimate(flops=2 * total * width * n, bytes_accessed=16 << 20, transcendentals=0),
        name="ffn_backward",
    )(cot, act, pg, down)


def rms_inverse(values):
    return lax.rsqrt(jnp.mean(values * values, axis=-1, keepdims=True) + EPSILON)


def norm_backward(grad_normed, values, inv_rms, gain_row):
    scaled = grad_normed * gain_row
    inner_sum = jnp.mean(scaled * values, axis=-1, keepdims=True)
    return inv_rms * scaled - values * (inv_rms * inv_rms * inv_rms) * inner_sum


def mm(a, b):
    return dot_nn(a, b)


def mm_tn(a, b):
    return lax.dot_general(a, b, (((0,), (0,)), ((), ())), preferred_element_type=F32)


def local(tokens, cotangent, segment_ids, w_query, w_keyval, w_out, w_gate, w_up, w_down, norm_gains):
    nt = lax.axis_size("tensor")
    t, c = lax.axis_index("tensor"), lax.axis_index("context")
    tokens, cotangent = tokens[0], cotangent[0]
    own_rows, width = tokens.shape
    rows = own_rows * nt
    if rows != WINDOW:
        raise ValueError("shard length")
    order = tensor_order(nt)
    blocks = jnp.array(order, jnp.int32) ^ t

    part = w_keyval.shape[0]
    kv_cols = w_keyval.shape[1]
    nf, nc = lax.axis_size("fsdp"), lax.axis_size("context")
    small_own = jnp.concatenate([w_keyval, norm_gains.T, jnp.zeros((part, 126), BF)], axis=1)
    first_own = jnp.concatenate([w_query, small_own], axis=0)
    wo_own, wd_own = w_out.T, w_down.T
    slots = slots_of()
    both = ("fsdp", "context")

    first_along = along(first_own)
    first_early = across(first_own)
    token_blocks = tensor_blocks(tokens)
    first_along = along(first_own)
    first_early = across(first_own)
    token_blocks = tensor_blocks(tokens)
    wg = lax.all_gather(w_gate, both, axis=0, tiled=True)
    first_along = jnp.stack(first_along)
    first_across = across(first_along, first_early)
    gate_up = jnp.concatenate([w_gate, w_up, wd_own], axis=1)
    gate_up = lax.all_gather(after(gate_up, *first_along), both, axis=0, tiled=True)
    first_along = jnp.stack(first_along)
    first_across = across(first_along, first_early)
    wu = lax.all_gather(after(w_up, *first_across), both, axis=0, tiled=True)
    wo_along = along(wo_own, first_along)
    wo_all = jnp.stack([wo_own, *wo_along])
    wo_across = across(wo_all, first_across)

    own_rows_q = nt * part
    wq, small = place(slots, gathered(first_own, first_along, first_early, first_across), [(0, own_rows_q), (own_rows_q, own_rows_q + part)])
    small_blocks = tensor_blocks(small.reshape(nf * nc, part, -1))
    cot_blocks = tensor_blocks(cotangent, small_blocks)
    small = jnp.zeros((nf * nc, nt, part, small.shape[1]), BF)
    for i in range(nt):
        small = lax.dynamic_update_index_in_dim(small, small_blocks[i], t ^ order[i], 1)
    small = small.reshape(width, -1)
    wkv = small[:, :kv_cols]
    gain_cols = small[:, kv_cols : kv_cols + 2].astype(F32)
    gains = gain_cols.T
    gain_one, gain_two = gains[0:1], gains[1:2]

    ids = segment_ids[0]
    own_seg = lax.dynamic_slice_in_dim(ids, c * rows, rows, 0)
    prev_seg = lax.dynamic_slice_in_dim(ids, jnp.maximum(c - 1, 0) * rows, rows, 0)
    prev_seg = jnp.where(c > 0, prev_seg, -1)
    qseg = own_seg[None, :]
    kseg = jnp.broadcast_to(jnp.concatenate([prev_seg, own_seg])[:, None], (2 * rows, 128))

    xin = jnp.concatenate(token_blocks, axis=0).astype(F32)
    inv_one_rows = rms_inverse(xin)
    normed_one = (xin * inv_one_rows * gain_one).astype(BF)
    keyvals = mm(normed_one, wkv).astype(BF)
    earlier = shift(keyvals, "context", 1)
    queries = mm(normed_one, wq).astype(BF)
    heads_out, lse = attention_forward(blocks, after(queries, cot_blocks[1]), earlier, keyvals, qseg, kseg, nt)
    (wo_t,) = place(slots, [wo_all] + behind(wo_across, heads_out))
    heads_now = heads_out
    branch = reduce_tensor(lambda i, j: dot_nt(heads_now[i:j], wo_t), rows)
    own_in = tokens.astype(F32)
    middle = own_in + branch
    inv_two = rms_inverse(middle)
    normed_two = (middle * inv_two * gain_two).astype(BF)
    second_blocks = tensor_blocks(normed_two)

    hidden, act, pg, second_rows, cot_rows = ffn_forward(second_blocks, cot_blocks, gate_up)
    part_down = slabs_of(mm_tn(cot_rows, hidden).astype(BF))
    got_down = half_sent(part_down)
    grads = ffn_backward(after(cot_rows, part_down), act, pg, gate_up, nt)
    ff = w_gate.shape[1]
    gate_up, wd_t = gate_up[:, : 2 * ff], gate_up[:, 2 * ff :]
    half = rows // 2
    two_away = dot_nt(grads[half:], gate_up).astype(BF)
    two_own = dot_nt(grads[:half], gate_up)
    d_two = reduce_halves(two_away, two_own)
    part_gate = slabs_of(mm_tn(after(second_rows, two_away, two_own), grads[:, :ff]).astype(BF))
    got_down = behind(got_down, part_gate)
    grad_down = rest_large(half_sum(part_down, got_down))
    sent_gate = behind(away_half(part_gate), *got_down)
    got_gate = [swap(x, "context", k + 1) for k, x in enumerate(sent_gate)]
    part_up = slabs_of(mm_tn(after(second_rows, *sent_gate), grads[:, ff:]).astype(BF))

    gain_two_part = jnp.sum(d_two * middle * inv_two, axis=0, keepdims=True)
    d_middle = cotangent.astype(F32) + norm_backward(d_two, middle, inv_two, gain_two)
    back_blocks = tensor_blocks(d_middle.astype(BF))
    hidden = after(hidden, back_blocks[1])
    ffn = reduce_tensor(lambda i, j: dot_nt(hidden[i:j], wd_t), rows)
    output = (middle + ffn).astype(BF)
    back_rows = jnp.concatenate(back_blocks, axis=0)
    got_gate = behind(got_gate, part_up)
    grad_gate = rest_large(half_sum(part_gate, got_gate))
    got_up = half_sent(part_up, got_gate)
    d_head = mm(after(back_rows, *got_gate), wo_t).astype(BF)
    dq, dboth = attention_backward(blocks, queries, earlier, keyvals, qseg, kseg, d_head, lse, nt)
    dboth = reduce_halves(dboth[rows // 2 :], dboth[: rows // 2].astype(F32))
    later = shift(dboth[:, :kv_cols].astype(BF), "context", -1)
    dkv = (dboth[:, kv_cols:] + later.astype(F32)).astype(BF)
    got_up = behind(got_up, dq)
    part_out = slabs_of(mm_tn(after(back_rows, dq), heads_out).astype(BF))

    d_one = reduce_tensor(lambda i, j: dot_nt(dq[i:j], wq), rows) + dot_nt(dkv, wkv)
    inv_one = rms_inverse(own_in)
    input_grad = d_middle + norm_backward(d_one, own_in, inv_one, gain_one)

    query_part = mm_tn(normed_one, dq)
    kv_part = mm_tn(normed_one[:own_rows], dkv)
    gain_one_part = jnp.sum(query_part * wq.astype(F32), axis=1, keepdims=True) + jnp.sum(kv_part * wkv.astype(F32), axis=1, keepdims=True)
    gain_one_part = gain_one_part / gain_cols[:, 0:1]
    small_part = jnp.concatenate([kv_part, gain_one_part, gain_two_part.T, jnp.zeros((width, 126), F32)], axis=1)
    small_part = small_part.reshape(-1, nt, part, kv_cols + 128)
    small_part = jnp.stack([lax.dynamic_index_in_dim(small_part, t ^ k, 1, False) for k in order])
    small_part = after(small_part, *got_up)
    small_part = reduce_tensor(lambda i, j: small_part[i:j], nt)[0].astype(BF)
    last = jnp.concatenate([slabs_of(query_part.astype(BF)), part_out], axis=2)
    got_last = half_sent(last, got_up)
    grad_up = rest_large(half_sum(part_up, got_up))
    small_part = small_part.reshape(nf, nc, part, kv_cols + 128)
    got_small = half_sent(small_part)
    small_sum, back = rest_small(half_sum(small_part, got_small))
    last, _ = rest_small(half_sum(last, got_last), back)
    grad_query, grad_out = last[: nt * part], last[nt * part :]
    grad_keyval = small_sum[:, :kv_cols]
    grad_gains = small_sum[:, kv_cols : kv_cols + 2].T
    return (output[None], input_grad[None], grad_query, grad_keyval, grad_out.T, grad_gate, grad_up, grad_down.T, grad_gains)


def solution(mesh):
    rows = P("fsdp", ("context", "tensor"), None)
    column = P(("fsdp", "context"), "tensor")
    row = P("tensor", ("fsdp", "context"))
    small = P(("fsdp", "context", "tensor"), None)
    gains = P(None, ("fsdp", "context", "tensor"))
    return jax.shard_map(
        local,
        mesh=mesh,
        in_specs=(rows, rows, P("fsdp", None), column, small, row, column, column, row, gains),
        out_specs=(rows, rows, column, small, row, column, column, row, gains),
        check_vma=False,
    )
```
